256 devices in a mesh: row: 4 (over y), col: 8 (over z), depth: 8 (over x, core).
Axes of the slice: x: 4, y: 4, z: 8, core: 2. Of those that a mesh axis runs over, the one named last changes fastest.
Arguments:
- tokens: bfloat16 [1024, 8192], P(('row', 'col'), 'depth'), may hold values from -6 to 6
- grad_out: bfloat16 [1024, 8192], P(('row', 'col'), 'depth'), may hold values from -6 to 6
- w_gate: bfloat16 [8192, 16384], P('depth', ('row', 'col')), may hold values from -0.0625 to 0.0625
- w_up: bfloat16 [8192, 16384], P('depth', ('row', 'col')), may hold values from -0.0625 to 0.0625
- w_down: bfloat16 [16384, 8192], P(('row', 'col'), 'depth'), may hold values from -0.046875 to 0.046875
- exp_gate: int32 [16384], P(('row', 'col')), may hold values from -6 to -4
- exp_up: int32 [16384], P(('row', 'col')), may hold values from -6 to -4
- exp_down: int32 [8192], P('depth'), may hold values from -6 to -4
- mask_gate: int32 [64, 128], P('depth', ('row', 'col')), may hold values 0 or 1
- mask_up: int32 [64, 128], P('depth', ('row', 'col')), may hold values 0 or 1
- mask_down: int32 [128, 64], P(('row', 'col'), 'depth'), may hold values 0 or 1
Outputs:
- out: bfloat16 [1024, 8192], P(('row', 'col'), 'depth')
- grad_tokens: bfloat16 [1024, 8192], P(('row', 'col'), 'depth')
- grad_gate: float32 [8192, 16384], P('depth', ('row', 'col'))
- grad_up: float32 [8192, 16384], P('depth', ('row', 'col'))
- grad_down: float32 [16384, 8192], P(('row', 'col'), 'depth')
The draws below stay inside these ranges and needn't reach their ends.
All inputs are finite; a program needn't handle non-finite values. No bound on the sum of `mask_gate` or of `mask_up` or of `mask_down` on one device may be relied on, other than what follows from the above.
Results may differ from the reference program's by a relative error of at most 0.006.
Values may be sent and summed in bfloat16 or wider, within the bound.
No kernel may reach another device: no remote copies, remote signals or barrier semaphores. Data moves between devices by JAX's collectives and lax.ppermute only.
A program may use at most 128 MiB of HBM per device.

```python
import jax
import jax.numpy as jnp

D = 8192
F = 16384
TILE = 128
TOKENS = 1024


def plant(result, rng, smallest, high):
    dims = result.shape
    spot = [jax.random.randint(jax.random.fold_in(rng, axis), (), 0, dims[axis]) for axis in range(len(dims))]
    result = result.at[tuple(spot)].set(smallest)
    longest = dims.index(max(dims))
    spot[longest] = (spot[longest] + 1) % dims[longest]
    return result.at[tuple(spot)].set(high)


def levels(stream_key, extent, split, least, largest):
    level = 1.0
    for dim, blocks in split:
        steps = jax.random.uniform(jax.random.fold_in(jax.random.fold_in(stream_key, 6), dim), (blocks,), jnp.float32, least / len(split), largest / len(split))
        level = level * jnp.repeat(jnp.exp(steps), extent[dim] // blocks).reshape((-1,) + (1,) * (len(extent) - 1 - dim))
    return level


def scatter_about(key, dims, scale, most, split=(), kind=jnp.bfloat16):
    gain = levels(key, dims, split, -0.22, 0.18) if split else 1.0
    values = jax.random.normal(key, dims, jnp.float32) * scale * gain
    return jnp.minimum(jnp.maximum(values, -most), most).astype(kind)


def setup_inputs(seed: int = 0) -> dict:
    key_of = jax.random.split(jax.random.key(seed), 12)
    tokens = scatter_about(key_of[0], (TOKENS, D), 1.0, 6.0, ((0, 32), (1, 8)))
    grad_out = scatter_about(key_of[1], (TOKENS, D), 1.0, 6.0, ((0, 32), (1, 8)))
    w_gate = scatter_about(key_of[2], (D, F), D ** -0.5, 0.0625, ((0, 8), (1, 32)))
    w_up = scatter_about(key_of[3], (D, F), D ** -0.5, 0.0625, ((0, 8), (1, 32)))
    w_down = scatter_about(key_of[4], (F, D), F ** -0.5, 0.046875, ((0, 32), (1, 8)))
    exp_gate = plant(jax.random.randint(key_of[5], (F,), -6, -3), jax.random.fold_in(key_of[5], 1), -6, (-3) - 1).astype(jnp.int32)
    exp_up = plant(jax.random.randint(key_of[6], (F,), -6, -3), jax.random.fold_in(key_of[6], 1), -6, (-3) - 1).astype(jnp.int32)
    exp_down = plant(jax.random.randint(key_of[7], (D,), -6, -3), jax.random.fold_in(key_of[7], 1), -6, (-3) - 1).astype(jnp.int32)
    mask_gate = plant((jax.random.randint(key_of[8], (D // TILE, F // TILE), 0, 2) < 1).astype(jnp.int32), jax.random.fold_in(key_of[8], 1), 0, 1)
    mask_up = plant((jax.random.randint(key_of[9], (D // TILE, F // TILE), 0, 2) < 1).astype(jnp.int32), jax.random.fold_in(key_of[9], 1), 0, 1)
    mask_down = plant((jax.random.randint(key_of[10], (F // TILE, D // TILE), 0, 2) < 1).astype(jnp.int32), jax.random.fold_in(key_of[10], 1), 0, 1)
    return {"tokens": tokens, "grad_out": grad_out, "w_gate": w_gate, "w_up": w_up, "w_down": w_down, "exp_gate": exp_gate, "exp_up": exp_up, "exp_down": exp_down, "mask_gate": mask_gate, "mask_up": mask_up, "mask_down": mask_down}


def spread_mask(mask):
    tile_rows, tile_cols = mask.shape
    wide = jnp.broadcast_to(mask.astype(jnp.float32)[:, None, :, None], (tile_rows, TILE, tile_cols, TILE))
    return wide.reshape(tile_rows * TILE, tile_cols * TILE)


def quantize(weight, exponent, mask, fan_in):
    offset = float(fan_in.bit_length() // 2)
    scale = jnp.exp2(exponent.astype(jnp.float32) - offset)[None, :]
    ratio = weight.astype(jnp.float32) / scale
    keep = spread_mask(mask)
    inside = (jnp.abs(ratio) <= 127.0).astype(jnp.float32) * keep
    coded = (jnp.clip(ratio, -127.0, 127.0) * scale * keep).astype(jnp.bfloat16)
    return coded, inside


def reference(tokens, grad_out, w_gate, w_up, w_down, exp_gate, exp_up, exp_down, mask_gate, mask_up, mask_down):
    q_gate, pass_gate = quantize(w_gate, exp_gate, mask_gate, D)
    q_up, pass_up = quantize(w_up, exp_up, mask_up, D)
    q_down, pass_down = quantize(w_down, exp_down, mask_down, F)
    gate = jnp.dot(tokens, q_gate, preferred_element_type=jnp.float32)
    up = jnp.dot(tokens, q_up, preferred_element_type=jnp.float32)
    sig = jax.nn.sigmoid(gate)
    act = (gate * sig * up).astype(jnp.bfloat16)
    out = jnp.dot(act, q_down, preferred_element_type=jnp.float32).astype(jnp.bfloat16)
    d_act = jnp.dot(grad_out, q_down.T, preferred_element_type=jnp.float32)
    d_gate = (d_act * up * sig * (1.0 + gate * (1.0 - sig))).astype(jnp.bfloat16)
    d_up = (d_act * gate * sig).astype(jnp.bfloat16)
    grad_tokens = (jnp.dot(d_gate, q_gate.T, preferred_element_type=jnp.float32)
                   + jnp.dot(d_up, q_up.T, preferred_element_type=jnp.float32)).astype(jnp.bfloat16)
    grad_gate = jnp.dot(tokens.T, d_gate, preferred_element_type=jnp.float32) * pass_gate
    grad_up = jnp.dot(tokens.T, d_up, preferred_element_type=jnp.float32) * pass_up
    grad_down = jnp.dot(act.T, grad_out, preferred_element_type=jnp.float32) * pass_down
    return (out, grad_tokens, grad_gate, grad_up, grad_down)
```

```python
import jax
import jax.numpy as jnp
from jax import lax
from jax.sharding import PartitionSpec as P

D = 8192
F = 16384
TILE = 128
BF16 = jnp.bfloat16
F32 = jnp.float32
CORE_WIRE = F32
FIRST_WIRE = BF16
SECOND_WIRE = F32


def spread_mask(mask):
    tile_rows, tile_cols = mask.shape
    wide = jnp.broadcast_to(
        mask.astype(jnp.float32)[:, None, :, None], (tile_rows, TILE, tile_cols, TILE)
    )
    return wide.reshape(tile_rows * TILE, tile_cols * TILE)


def quantize(weight, exponent, mask, fan_in):
    offset = float(fan_in.bit_length() // 2)
    scale = jnp.exp2(exponent.astype(jnp.float32) - offset)[None, :]
    ratio = weight.astype(jnp.float32) / scale
    keep = spread_mask(mask)
    inside = (jnp.abs(ratio) <= 127.0).astype(jnp.float32) * keep
    coded = (jnp.clip(ratio, -127.0, 127.0) * scale * keep).astype(jnp.bfloat16)
    return (coded, inside)


def dot(left, right, left_dim, right_dim):
    return lax.dot_general(
        left, right, (((left_dim,), (right_dim,)), ((), ())), preferred_element_type=F32
    )


def shift(block, axis, step):
    if axis == "x":
        pairs = [(i, ((i // 2 + step) % 4) * 2 + i % 2) for i in range(8)]
        return lax.ppermute(block, "depth", pairs)
    if axis == "core":
        return lax.ppermute(block, "depth", [(i, i ^ 1) for i in range(8)])
    size = lax.axis_size(axis)
    return lax.ppermute(block, axis, [(i, (i + step) % size) for i in range(size)])


def gather_ring(block, axis, size, halves):
    ahead, behind = [], []
    down = up = block
    for _ in range(size // 2 - 1):
        down = shift(down, axis, -1)
        up = shift(up, axis, 1)
        ahead.append(down)
        behind.append(up)
    if halves:
        half = block.shape[0] // 2
        far = jnp.concatenate([shift(down[:half], axis, -1), shift(up[half:], axis, 1)], axis=0)
    else:
        far = shift(down, axis, -1)
    return [block, *ahead, far, *reversed(behind)]


def scatter_ring(parts, axis, wire):
    size = len(parts)
    far = size // 2
    half = parts[0].shape[0] // 2
    up = shift(parts[far][:half].astype(wire), axis, 1).astype(F32)
    down = shift(parts[far][half:].astype(wire), axis, -1).astype(F32)
    for k in range(far - 1, 0, -1):
        a, b = parts[k], parts[size - k]
        if k == far - 1:
            a = jnp.concatenate([a[:half] + up, a[half:]], axis=0)
            b = jnp.concatenate([b[:half], b[half:] + down], axis=0)
        else:
            a, b = a + up, b + down
        up = shift(a.astype(wire), axis, 1).astype(F32)
        down = shift(b.astype(wire), axis, -1).astype(F32)
    return parts[0] + up + down


def scatter_x(halves, x):
    def at(k):
        return lax.dynamic_index_in_dim(halves, (x + k) % 4, 0, keepdims=False)

    return scatter_ring([at(k) for k in range(4)], "x", FIRST_WIRE)


def unit_backward(d_act, gate, up, sig):
    d_gate = (d_act * up * sig * (1.0 + gate * (1.0 - sig))).astype(jnp.bfloat16)
    d_up = (d_act * gate * sig).astype(jnp.bfloat16)
    return (d_gate, d_up)


def shards(
    tokens,
    grad_out,
    w_gate,
    w_up,
    w_down,
    exp_gate,
    exp_up,
    exp_down,
    mask_gate,
    mask_up,
    mask_down,
):
    depth = lax.axis_index("depth")
    x, core = depth // 2, depth % 2
    q_gate, pass_gate = quantize(w_gate, exp_gate, mask_gate, D)
    q_up, pass_up = quantize(w_up, exp_up, mask_up, D)
    q_down, pass_down = quantize(w_down, exp_down, mask_down, F)

    wide = jnp.concatenate(gather_ring(tokens, "col", 8, False), axis=0)
    all_tokens = jnp.concatenate(gather_ring(wide, "row", 4, True), axis=0)
    tall = jnp.stack(gather_ring(grad_out, "row", 4, False), axis=0)
    all_grad = jnp.stack(gather_ring(tall, "col", 8, True), axis=1).reshape(1024, 1024)

    def partial(start):
        t = lax.dynamic_slice_in_dim(all_tokens, start, 512, 0)
        g = lax.dynamic_slice_in_dim(all_grad, start, 512, 0)
        return jnp.concatenate(
            [dot(t, q_gate, 1, 0), dot(t, q_up, 1, 0), dot(g, q_down, 1, 1)], axis=1
        )

    sent = shift(partial((1 - core) * 512).astype(CORE_WIRE), "core", 1)
    chip = partial(core * 512) + sent.astype(F32)
    total = scatter_x(chip.reshape(4, 128, 1536), x)
    gate, up, d_act = total[:, :512], total[:, 512:1024], total[:, 1024:]
    sig = jax.nn.sigmoid(gate)
    act = (gate * sig * up).astype(BF16)
    d_gate, d_up = unit_backward(d_act, gate, up, sig)
    own = jnp.concatenate([act, d_gate, d_up], axis=1)
    blocks = jnp.concatenate(gather_ring(own, "x", 4, True), axis=0)
    mine = jnp.concatenate([blocks, blocks], axis=0)
    mine = lax.dynamic_slice_in_dim(mine, ((4 - x) % 4) * 128, 512, 0)
    other = shift(mine, "core", 1)
    units = jnp.where(
        core == 0,
        jnp.concatenate([mine, other], axis=0),
        jnp.concatenate([other, mine], axis=0),
    )
    act, d_gate, d_up = units[:, :512], units[:, 512:1024], units[:, 1024:]

    out = dot(act, q_down, 1, 0)
    out = scatter_ring([out[256 * j : 256 * j + 256] for j in range(4)], "row", FIRST_WIRE)
    out = scatter_ring([out[32 * k : 32 * k + 32] for k in range(8)], "col", SECOND_WIRE)
    back = (dot(d_gate, q_gate, 1, 1) + dot(d_up, q_up, 1, 1)).reshape(4, 8, 32, 1024)
    back = scatter_ring([back[:, k] for k in range(8)], "col", FIRST_WIRE)
    back = scatter_ring([back[j] for j in range(4)], "row", SECOND_WIRE)
    grad_gate = dot(all_tokens, d_gate, 0, 0) * pass_gate
    grad_up = dot(all_tokens, d_up, 0, 0) * pass_up
    grad_down = dot(act, all_grad, 0, 0) * pass_down
    return (out.astype(BF16), back.astype(BF16), grad_gate, grad_up, grad_down)


def solution(mesh):
    in_specs = (
        P(("row", "col"), "depth"),
        P(("row", "col"), "depth"),
        P("depth", ("row", "col")),
        P("depth", ("row", "col")),
        P(("row", "col"), "depth"),
        P(("row", "col")),
        P(("row", "col")),
        P("depth"),
        P("depth", ("row", "col")),
        P("depth", ("row", "col")),
        P(("row", "col"), "depth"),
    )
    out_specs = (
        P(("row", "col"), "depth"),
        P(("row", "col"), "depth"),
        P("depth", ("row", "col")),
        P("depth", ("row", "col")),
        P(("row", "col"), "depth"),
    )
    return jax.shard_map(shards, mesh=mesh, in_specs=in_specs, out_specs=out_specs, check_vma=False)
```

```python
import jax
import jax.numpy as jnp
from jax import lax
from jax.experimental import pallas as pl
from jax.experimental.pallas import tpu as pltpu
from jax.sharding import PartitionSpec as P

D = 8192
F = 16384
TILE = 128
BF16 = jnp.bfloat16
F32 = jnp.float32


def limits(exponent, fan_in):
    offset = fan_in.bit_length() // 2
    scale = jnp.exp2(exponent.astype(F32) - float(offset))
    top = 127.0 / jnp.left_shift(1, offset - exponent).astype(F32)
    return top, jnp.where(jnp.abs(top / scale) <= 127.0, top, top * (1.0 - 2.0**-9))


def quantize_kernel(mask_gate, mask_up, mask_down, w_gate, w_up, w_down, bounds, coded, inside):
    def one(weight, mask, place, row, first):
        cols = weight.shape[1]

        def rows(i, carry):
            span = pl.ds(pl.multiple_of(i * TILE, TILE), TILE)
            into = pl.ds(pl.multiple_of(row + i * TILE, TILE), TILE)
            for j in range(cols // TILE):
                at = slice(j * TILE, (j + 1) * TILE)
                to = slice(first + j * TILE, first + (j + 1) * TILE)
                bound = slice(place + j * TILE, place + (j + 1) * TILE)
                keep = mask[i, j].astype(F32)
                w = weight[span, at].astype(F32)
                top, most = bounds[0:1, bound], bounds[1:2, bound]
                coded[into, to] = (jnp.clip(w, -top, top) * keep).astype(BF16)
                inside[into, to] = jnp.where(jnp.abs(w) <= most, keep, 0.0).astype(BF16)
            return carry

        lax.fori_loop(0, weight.shape[0] // TILE, rows, 0)

    cols = w_gate.shape[1]
    one(w_gate, mask_gate, 0, 0, 0)
    one(w_up, mask_up, cols, 0, cols)
    one(w_down, mask_down, 2 * cols, w_gate.shape[0], 0)


def quantize(w_gate, w_up, w_down, e_gate, e_up, e_down, mask_gate, mask_up, mask_down):
    both = jax.ShapeDtypeStruct((w_gate.shape[0] + w_down.shape[0], w_down.shape[1]), BF16)
    found = [limits(e_gate, D), limits(e_up, D), limits(e_down, F)]
    bounds = jnp.stack([jnp.concatenate(row) for row in zip(*found)])
    smem = pl.BlockSpec(memory_space=pltpu.SMEM)
    vmem = pl.BlockSpec(memory_space=pltpu.VMEM)
    return pl.pallas_call(
        quantize_kernel,
        out_shape=(both, both),
        in_specs=[smem] * 3 + [vmem] * 4,
        out_specs=(vmem, vmem),
        compiler_params=pltpu.CompilerParams(vmem_limit_bytes=32 << 20),
    )(mask_gate, mask_up, mask_down, w_gate, w_up, w_down, bounds)


def dot(left, right, left_dim, right_dim):
    return lax.dot_general(
        left, right, (((left_dim,), (right_dim,)), ((), ())), preferred_element_type=F32
    )


def shift(block, axis, step):
    if axis == "x":
        pairs = [(i, ((i // 2 + step) % 4) * 2 + i % 2) for i in range(8)]
        return lax.ppermute(block, "depth", pairs)
    size = lax.axis_size(axis)
    return lax.ppermute(block, axis, [(i, (i + step) % size) for i in range(size)])


def swap(block):
    return lax.ppermute(block, "depth", [(i, i ^ 1) for i in range(8)])


def after(value, *others):
    return lax.optimization_barrier((value, *others))[0]


def split_ways(block, axis, step):
    size = 4 if axis == "x" else lax.axis_size(axis)
    if axis == "x":
        pairs = [(i, ((i // 2 + (-step if i % 2 else step)) % 4) * 2 + i % 2) for i in range(8)]
        return lax.ppermute(block, "depth", pairs)
    pairs = [
        (i * 8 + d, (i + (-step if d % 2 else step)) % size * 8 + d)
        for i in range(size)
        for d in range(8)
    ]
    return lax.ppermute(block, (axis, "depth"), pairs)


def together(*values):
    return lax.optimization_barrier(values)


def gather_x(block, core):
    ahead, behind = shift(block, "x", -1), shift(block, "x", 1)
    far = split_ways(jnp.where(core == 0, behind, ahead), "x", 1)
    return [block, ahead, far, behind]


def scatter_x(parts, core):
    got = split_ways(parts[2].astype(BF16), "x", 1).astype(F32)
    up, down = jnp.where(core == 0, got, 0.0), jnp.where(core == 0, 0.0, got)
    up = shift((parts[1] + up).astype(BF16), "x", 1).astype(F32)
    down = shift((parts[3] + down).astype(BF16), "x", -1).astype(F32)
    return parts[0] + up + down


def rolled(core, blocks, turn):
    return jnp.where(core == 0, blocks, jnp.concatenate([blocks[turn:], blocks[:turn]]))


def gather(own_t, own_g, core, x):
    slabs = own_t.shape[1]
    t4 = shift(own_t, "col", 4)
    near = [own_g, shift(own_g, "row", -1), shift(own_g, "row", 2), shift(own_g, "row", 1)]
    tall = jnp.zeros((4, 16, slabs), BF16)
    for j, block in enumerate(near):
        tall = lax.dynamic_update_slice(tall, block[None], ((j - x) % 4, 0, 0))
    t4, tall = together(t4, tall)
    pair = jnp.stack([own_t, t4])
    got = split_ways(pair, "col", -2)
    g1, g7 = shift(tall, "col", -1), shift(tall, "col", 1)
    got, g1, g7 = together(got, g1, g7)
    got = rolled(core, got, 1)
    even = jnp.stack([pair[0], got[0], pair[1], got[1]])
    odd = split_ways(even, "col", -1)
    g2, g6 = shift(g1, "col", -1), shift(g7, "col", 1)
    odd, g2, g6 = together(odd, g2, g6)
    wide = jnp.stack([even, rolled(core, odd, 1)], axis=1).reshape(128, slabs)
    t1, t3 = shift(wide, "row", -1), shift(wide, "row", 1)
    g3, g5 = shift(g2, "col", -1), shift(g6, "col", 1)
    t2 = split_ways(jnp.where(core == 0, t3, t1), "row", 1)
    g4 = split_ways(jnp.where(core == 0, g5, g3), "col", 1)
    all_t = jnp.zeros((4, 128, slabs), BF16)
    for j, block in enumerate([wide, t1, t2, t3]):
        all_t = lax.dynamic_update_slice(all_t, block[None], ((j - x) % 4, 0, 0))
    all_g = jnp.stack([tall, g1, g2, g3, g4, g5, g6, g7], axis=1)
    return all_t.reshape(512, slabs), all_g.reshape(512, slabs), wide


def scatter(out, back, core, x, units, far_units, grads):
    def send(part, axis, step, wire=BF16):
        return shift(part.astype(wire), axis, step).astype(F32)

    def send_split(part, axis, step):
        return split_ways(part.astype(BF16), axis, step).astype(F32)

    def ways(got):
        return jnp.where(core == 0, got, 0.0), jnp.where(core == 0, 0.0, got)

    o, b = together(send_split(out[2], "row", 1), send_split(back[4], "col", 1))
    o1, o3 = ways(o)
    b1, b7 = ways(b)
    o1, o3 = send(out[1] + o1, "row", 1), send(out[3] + o3, "row", -1)
    b1, b7 = send(back[3] + b1, "col", 1), send(back[5] + b7, "col", -1)
    o1, o3, units, far_units = together(o1, o3, units, far_units)
    sums = (out[0] + o1 + o3).reshape(4, 2, 16, out[0].shape[1])
    even, odd = sums[:, 0], sums[:, 1]
    got = send_split(rolled(core, odd, 3), "col", 1)
    b1, b7 = send(back[2] + b1, "col", 1), send(back[6] + b7, "col", -1)
    grad_gate = grads[0](units, far_units)
    got, b1, b7, grad_gate, units, far_units = together(got, b1, b7, grad_gate, units, far_units)
    even = even + got
    near, two = even[::2], even[1::2]
    got = send_split(rolled(core, two, 1), "col", 2)
    b1, b7 = send(back[1] + b1, "col", 1), send(back[7] + b7, "col", -1)
    grad_up = grads[1](units, far_units)
    got, b1, b7, grad_up, units, far_units = together(got, b1, b7, grad_up, units, far_units)
    near = near + got
    out = near[0] + send(near[1], "col", 4)
    back = back[0] + b1 + b7
    parts = [lax.dynamic_index_in_dim(back, (j - x) % 4, 0, keepdims=False) for j in range(4)]
    back = (
        parts[0]
        + send(parts[1], "row", 1, F32)
        + send(parts[3], "row", -1, F32)
        + send(parts[2], "row", 2, F32)
    )
    grad_down = grads[2](units, far_units)
    out, back, grad_down = together(out, back, grad_down)
    return out, back, (grad_gate, grad_up, grad_down)


def unit_backward(d_act, gate, up, sig):
    d_gate = (d_act * up * sig * (1.0 + gate * (1.0 - sig))).astype(jnp.bfloat16)
    d_up = (d_act * gate * sig).astype(jnp.bfloat16)
    return (d_gate, d_up)


def shards(
    tokens,
    grad_out,
    w_gate,
    w_up,
    w_down,
    exp_gate,
    exp_up,
    exp_down,
    mask_gate,
    mask_up,
    mask_down,
):
    depth = lax.axis_index("depth")
    x, core = depth // 2, depth % 2
    slab = tokens.shape[1]

    pair = jnp.concatenate([tokens, grad_out], axis=1)
    kept = lax.dynamic_slice_in_dim(pair, core * 16, 16, 0)
    got = swap(lax.dynamic_slice_in_dim(pair, (1 - core) * 16, 16, 0))
    own_t = jnp.concatenate([kept[:, :slab], got[:, :slab]], axis=1)
    own_g = jnp.concatenate([kept[:, slab:], got[:, slab:]], axis=1)

    all_t, all_g, wide = gather(own_t, own_g, core, x)

    weights = together(
        w_gate, w_up, w_down, exp_gate, exp_up, exp_down, mask_gate, mask_up, mask_down, wide
    )[:-1]
    coded, inside = quantize(*weights)
    coded_far = swap(coded)
    near_t, near_g = all_t[:, :slab], all_g[:, :slab]
    far_tg = swap(jnp.concatenate([all_t[:, slab:], all_g[:, slab:]], axis=0))

    def partial(first, rows):
        t, g = all_t[first : first + rows], all_g[first : first + rows]
        gate_up = dot(t[:, :slab], coded[:slab], 1, 0) + dot(t[:, slab:], coded_far[:slab], 1, 0)
        d_act = dot(g[:, :slab], coded[slab:], 1, 1) + dot(g[:, slab:], coded_far[slab:], 1, 1)
        return gate_up, d_act

    far_part = jnp.concatenate(partial(256, 128), axis=1)
    gate_up, d_act = partial(0, 512)
    parts = [
        jnp.concatenate([gate_up[s : s + 128], d_act[s : s + 128]], axis=1) for s in (0, 128, 384)
    ]
    total = scatter_x([*parts[:2], far_part, parts[2]], core)
    total = after(total, far_tg)
    gate, up, d_act = total[:, :512], total[:, 512:1024], total[:, 1024:]
    sig = jax.nn.sigmoid(gate)
    act = (gate * sig * up).astype(BF16)
    d_gate, d_up = unit_backward(d_act, gate, up, sig)
    own = jnp.concatenate([act, d_gate, d_up], axis=1)
    units = jnp.concatenate(gather_x(own, core), axis=0)

    far_units = swap(units)

    def out_part(j):
        rows = lax.dynamic_slice_in_dim(units[:, :512], ((j - x) % 4) * 128, 128, 0)
        return jnp.concatenate(
            [dot(rows, coded[slab:], 1, 0), dot(rows, coded_far[slab:], 1, 0)], axis=1
        )

    def back_part(rows):
        return jnp.concatenate(
            [dot(rows, coded[:slab], 1, 1), dot(rows, coded_far[:slab], 1, 1)], axis=1
        )

    both = units[:, 512:]
    back_far = back_part(both.reshape(4, 8, 16, 1024)[:, 4].reshape(64, 1024))
    back = back_part(both).reshape(4, 8, 16, 2 * slab)
    back = [back[:, k] for k in range(8)]
    back[4] = back_far.reshape(4, 16, 2 * slab)

    far_t, far_g = far_tg[:512], far_tg[512:]

    def unit_grad(columns, mask):
        def grad(units, far_units):
            sums = dot(near_t, units[:, columns], 0, 0) + dot(far_t, far_units[:, columns], 0, 0)
            return sums * mask.astype(F32)

        return grad

    def down_grad(units, far_units):
        sums = dot(units[:, :512], near_g, 0, 0) + dot(far_units[:, :512], far_g, 0, 0)
        return sums * inside[slab:].astype(F32)

    out, back, grads = scatter(
        [out_part(j) for j in range(4)],
        back,
        core,
        x,
        units,
        far_units,
        [
            unit_grad(slice(512, 1024), inside[:slab, :512]),
            unit_grad(slice(1024, 1536), inside[:slab, 512:]),
            down_grad,
        ],
    )

    out, back = out.astype(BF16), back.astype(BF16)
    got = swap(jnp.concatenate([out[:, slab:], back[:, slab:]], axis=1))

    def finish(mine, other):
        return jnp.where(
            core == 0,
            jnp.concatenate([mine, other], axis=0),
            jnp.concatenate([other, mine], axis=0),
        )

    out = finish(out[:, :slab], got[:, :slab])
    back = finish(back[:, :slab], got[:, slab:])
    return (out, back, *grads)


def solution(mesh):
    in_specs = (
        P(("row", "col"), "depth"),
        P(("row", "col"), "depth"),
        P("depth", ("row", "col")),
        P("depth", ("row", "col")),
        P(("row", "col"), "depth"),
        P(("row", "col")),
        P(("row", "col")),
        P("depth"),
        P("depth", ("row", "col")),
        P("depth", ("row", "col")),
        P(("row", "col"), "depth"),
    )
    out_specs = (
        P(("row", "col"), "depth"),
        P(("row", "col"), "depth"),
        P("depth", ("row", "col")),
        P("depth", ("row", "col")),
        P(("row", "col"), "depth"),
    )
    return jax.shard_map(shards, mesh=mesh, in_specs=in_specs, out_specs=out_specs, check_vma=False)
```

```python
import jax
import jax.numpy as jnp
from jax import lax
from jax.experimental import pallas as pl
from jax.experimental.pallas import tpu as pltpu
from jax.sharding import PartitionSpec as P

D = 8192
F = 16384
TILE = 128
BF16 = jnp.bfloat16
F32 = jnp.float32


def limits(exponent, fan_in):
    offset = fan_in.bit_length() // 2
    scale = jnp.exp2(exponent.astype(F32) - float(offset))
    top = 127.0 / jnp.left_shift(1, offset - exponent).astype(F32)
    return top, jnp.where(jnp.abs(top / scale) <= 127.0, top, top * (1.0 - 2.0**-9))


def quantize_kernel(mask_gate, mask_up, mask_down, w_gate, w_up, w_down, bounds, coded, inside):
    def one(weight, mask, place, row, first):
        cols = weight.shape[1]

        def rows(i, carry):
            span = pl.ds(pl.multiple_of(i * TILE, TILE), TILE)
            into = pl.ds(pl.multiple_of(row + i * TILE, TILE), TILE)
            for j in range(cols // TILE):
                at = slice(j * TILE, (j + 1) * TILE)
                to = slice(first + j * TILE, first + (j + 1) * TILE)
                bound = slice(place + j * TILE, place + (j + 1) * TILE)
                keep = mask[i, j].astype(F32)
                w = weight[span, at].astype(F32)
                top, most = bounds[0:1, bound], bounds[1:2, bound]
                coded[into, to] = (jnp.clip(w, -top, top) * keep).astype(BF16)
                inside[into, to] = jnp.where(jnp.abs(w) <= most, keep, 0.0).astype(BF16)
            return carry

        lax.fori_loop(0, weight.shape[0] // TILE, rows, 0)

    cols = w_gate.shape[1]
    one(w_gate, mask_gate, 0, 0, 0)
    one(w_up, mask_up, cols, 0, cols)
    one(w_down, mask_down, 2 * cols, w_gate.shape[0], 0)


def quantize(w_gate, w_up, w_down, e_gate, e_up, e_down, mask_gate, mask_up, mask_down):
    both = jax.ShapeDtypeStruct((w_gate.shape[0] + w_down.shape[0], w_down.shape[1]), BF16)
    found = [limits(e_gate, D), limits(e_up, D), limits(e_down, F)]
    bounds = jnp.stack([jnp.concatenate(row) for row in zip(*found)])
    smem = pl.BlockSpec(memory_space=pltpu.SMEM)
    vmem = pl.BlockSpec(memory_space=pltpu.VMEM)
    return pl.pallas_call(
        quantize_kernel,
        out_shape=(both, both),
        in_specs=[smem] * 3 + [vmem] * 4,
        out_specs=(vmem, vmem),
        compiler_params=pltpu.CompilerParams(vmem_limit_bytes=32 << 20),
    )(mask_gate, mask_up, mask_down, w_gate, w_up, w_down, bounds)


def dot(left, right, left_dim, right_dim):
    return lax.dot_general(
        left, right, (((left_dim,), (right_dim,)), ((), ())), preferred_element_type=F32
    )


def shift(block, axis, step):
    if axis == "x":
        size, inner = 4, 2
        names = "depth"
    else:
        size, inner = lax.axis_size(axis), 8
        names = (axis, "depth")
    pairs = [
        (i * inner + d, (i + (-step if d % 2 else step)) % size * inner + d)
        for i in range(size)
        for d in range(inner)
    ]
    return lax.ppermute(block, names, pairs)


def swap(block):
    return lax.ppermute(block, "depth", [(i, i ^ 1) for i in range(8)])


def after(value, *others):
    return lax.optimization_barrier((value, *others))[0]


def together(*values):
    return lax.optimization_barrier(values)


def gather_x(block):
    ahead, behind = shift(block, "x", -1), shift(block, "x", 1)
    return [block, ahead, shift(behind, "x", 1), behind]


def scatter_x(parts):
    up = shift(parts[2].astype(BF16), "x", 1).astype(F32)
    up = shift((parts[1] + up).astype(BF16), "x", 1).astype(F32)
    down = shift(parts[3].astype(BF16), "x", -1).astype(F32)
    return parts[0] + up + down


def gather(own_t, own_g, place):
    slabs = own_t.shape[1]
    t4 = shift(own_t, "col", 4)
    near = [own_g, shift(own_g, "row", -1), shift(own_g, "row", 2), shift(own_g, "row", 1)]
    tall = jnp.zeros((4, 16, slabs), BF16)
    for j, block in enumerate(near):
        tall = lax.dynamic_update_slice(tall, block[None], (place[j], 0, 0))
    t4, tall = together(t4, tall)
    got = shift(jnp.stack([own_t, t4]), "col", -2)
    g1, g7 = shift(tall, "col", -1), shift(tall, "col", 1)
    got, g1, g7 = together(got, g1, g7)
    even = jnp.stack([own_t, got[0], t4, got[1]])
    odd = shift(even, "col", -1)
    g2, g6 = shift(g1, "col", -1), shift(g7, "col", 1)
    odd, g2, g6 = together(odd, g2, g6)
    wide = jnp.stack([even, odd], axis=1).reshape(128, slabs)
    t1, t3 = shift(wide, "row", -1), shift(wide, "row", 1)
    g3, g5 = shift(g2, "col", -1), shift(g6, "col", 1)
    t2, g4 = shift(t3, "row", 1), shift(g5, "col", 1)
    all_t = jnp.zeros((4, 128, slabs), BF16)
    for j, block in enumerate([wide, t1, t2, t3]):
        all_t = lax.dynamic_update_slice(all_t, block[None], (place[j], 0, 0))
    all_g = jnp.stack([tall, g1, g2, g3, g4, g5, g6, g7], axis=1)
    return all_t.reshape(512, slabs), all_g.reshape(512, slabs), (g3, g5)


def scatter(out, back, place, units, far_units, grads):
    def send(part, axis, step, wire=BF16):
        return shift(part.astype(wire), axis, step).astype(F32)

    o1, b1 = together(send(out[2], "row", 1), send(back[4], "col", 1))
    o1, o3 = send(out[1] + o1, "row", 1), send(out[3], "row", -1)
    b1, b7 = send(back[3] + b1, "col", 1), send(back[5], "col", -1)
    o1, o3, b1, b7, units, far_units = together(o1, o3, b1, b7, units, far_units)
    sums = (out[0] + o1 + o3).reshape(4, 2, 16, out[0].shape[1])
    got = send(sums[:, 1], "col", 1)
    b1, b7 = send(back[2] + b1, "col", 1), send(back[6] + b7, "col", -1)
    grad_gate = grads[0](units, far_units)
    got, b1, b7, grad_gate, units, far_units = together(got, b1, b7, grad_gate, units, far_units)
    even = sums[:, 0] + got
    got = send(even[1::2], "col", 2)
    b1, b7 = send(back[1] + b1, "col", 1), send(back[7] + b7, "col", -1)
    grad_up = grads[1](units, far_units)
    got, b1, b7, grad_up, units, far_units = together(got, b1, b7, grad_up, units, far_units)
    near = even[::2] + got
    out = near[0] + send(near[1], "col", 4)
    back = back[0] + b1 + b7
    parts = [lax.dynamic_index_in_dim(back, at, 0, keepdims=False) for at in place]
    back = (
        parts[0]
        + send(parts[1], "row", 1, F32)
        + send(parts[3], "row", -1, F32)
        + send(parts[2], "row", 2, F32)
    )
    grad_down = grads[2](units, far_units)
    out, back, grad_down = together(out, back, grad_down)
    return out, back, (grad_gate, grad_up, grad_down)


def unit_backward(d_act, gate, up, sig):
    d_gate = (d_act * up * sig * (1.0 + gate * (1.0 - sig))).astype(jnp.bfloat16)
    d_up = (d_act * gate * sig).astype(jnp.bfloat16)
    return (d_gate, d_up)


def shards(
    tokens,
    grad_out,
    w_gate,
    w_up,
    w_down,
    exp_gate,
    exp_up,
    exp_down,
    mask_gate,
    mask_up,
    mask_down,
):
    depth = lax.axis_index("depth")
    x, core = depth // 2, depth % 2
    slab = tokens.shape[1]

    pair = jnp.concatenate([tokens, grad_out], axis=1)
    kept = lax.dynamic_slice_in_dim(pair, core * 16, 16, 0)
    got = swap(lax.dynamic_slice_in_dim(pair, (1 - core) * 16, 16, 0))
    own_t = jnp.concatenate([kept[:, :slab], got[:, :slab]], axis=1)
    own_g = jnp.concatenate([kept[:, slab:], got[:, slab:]], axis=1)

    place = [(jnp.where(core == 0, j - x, x - j) + 4) % 4 for j in range(4)]
    all_t, all_g, late = gather(own_t, own_g, place)

    small = together(exp_gate, exp_up, exp_down, mask_gate, mask_up, mask_down, *late)[:6]
    coded, inside = quantize(w_gate, w_up, w_down, *small)
    coded_far = swap(coded)
    near_t, near_g = all_t[:, :slab], all_g[:, :slab]
    far_tg = swap(jnp.concatenate([all_t[:, slab:], all_g[:, slab:]], axis=0))

    def partial(first, rows):
        t, g = all_t[first : first + rows], all_g[first : first + rows]
        gate_up = dot(t[:, :slab], coded[:slab], 1, 0) + dot(t[:, slab:], coded_far[:slab], 1, 0)
        d_act = dot(g[:, :slab], coded[slab:], 1, 1) + dot(g[:, slab:], coded_far[slab:], 1, 1)
        return gate_up, d_act

    far_part = jnp.concatenate(partial(256, 128), axis=1)
    gate_up, d_act = partial(0, 512)
    parts = [
        jnp.concatenate([gate_up[s : s + 128], d_act[s : s + 128]], axis=1) for s in (0, 128, 384)
    ]
    total = scatter_x([*parts[:2], far_part, parts[2]])
    total = after(total, far_tg)
    gate, up, d_act = total[:, :512], total[:, 512:1024], total[:, 1024:]
    sig = jax.nn.sigmoid(gate)
    act = (gate * sig * up).astype(BF16)
    d_gate, d_up = unit_backward(d_act, gate, up, sig)
    own = jnp.concatenate([act, d_gate, d_up], axis=1)
    units = jnp.concatenate(gather_x(own), axis=0)

    far_units = swap(units)

    def out_part(j):
        rows = lax.dynamic_slice_in_dim(units[:, :512], place[j] * 128, 128, 0)
        return jnp.concatenate(
            [dot(rows, coded[slab:], 1, 0), dot(rows, coded_far[slab:], 1, 0)], axis=1
        )

    def back_part(rows):
        return jnp.concatenate(
            [dot(rows, coded[:slab], 1, 1), dot(rows, coded_far[:slab], 1, 1)], axis=1
        )

    both = units[:, 512:]
    back_far = back_part(both.reshape(4, 8, 16, 1024)[:, 4].reshape(64, 1024))
    back = back_part(both).reshape(4, 8, 16, 2 * slab)
    back = [back[:, k] for k in range(8)]
    back[4] = back_far.reshape(4, 16, 2 * slab)

    far_t, far_g = far_tg[:512], far_tg[512:]

    def unit_grad(columns, mask):
        def grad(units, far_units):
            sums = dot(near_t, units[:, columns], 0, 0) + dot(far_t, far_units[:, columns], 0, 0)
            return sums * mask.astype(F32)

        return grad

    def down_grad(units, far_units):
        sums = dot(units[:, :512], near_g, 0, 0) + dot(far_units[:, :512], far_g, 0, 0)
        return sums * inside[slab:].astype(F32)

    out, back, grads = scatter(
        [out_part(j) for j in range(4)],
        back,
        place,
        units,
        far_units,
        [
            unit_grad(slice(512, 1024), inside[:slab, :512]),
            unit_grad(slice(1024, 1536), inside[:slab, 512:]),
            down_grad,
        ],
    )

    out, back = out.astype(BF16), back.astype(BF16)
    got = swap(jnp.concatenate([out[:, slab:], back[:, slab:]], axis=1))

    def finish(mine, other):
        return jnp.where(
            core == 0,
            jnp.concatenate([mine, other], axis=0),
            jnp.concatenate([other, mine], axis=0),
        )

    out = finish(out[:, :slab], got[:, :slab])
    back = finish(back[:, :slab], got[:, slab:])
    return (out, back, *grads)


def solution(mesh):
    in_specs = (
        P(("row", "col"), "depth"),
        P(("row", "col"), "depth"),
        P("depth", ("row", "col")),
        P("depth", ("row", "col")),
        P(("row", "col"), "depth"),
        P(("row", "col")),
        P(("row", "col")),
        P("depth"),
        P("depth", ("row", "col")),
        P("depth", ("row", "col")),
        P(("row", "col"), "depth"),
    )
    out_specs = (
        P(("row", "col"), "depth"),
        P(("row", "col"), "depth"),
        P("depth", ("row", "col")),
        P("depth", ("row", "col")),
        P(("row", "col"), "depth"),
    )
    return jax.shard_map(shards, mesh=mesh, in_specs=in_specs, out_specs=out_specs, check_vma=False)
```

```python
import jax
import jax.numpy as jnp
from jax import lax
from jax.experimental import pallas as pl
from jax.experimental.pallas import tpu as pltpu
from jax.sharding import PartitionSpec as P

D = 8192
F = 16384
TILE = 128
BF16 = jnp.bfloat16
F32 = jnp.float32


def limits(exponent, fan_in):
    offset = fan_in.bit_length() // 2
    scale = jnp.exp2(exponent.astype(F32) - float(offset))
    top = 127.0 / jnp.left_shift(1, offset - exponent).astype(F32)
    return top, jnp.where(jnp.abs(top / scale) <= 127.0, top, top * (1.0 - 2.0**-9))


def quantize_kernel(mask_gate, mask_up, mask_down, w_gate, w_up, w_down, bounds, coded, inside):
    def one(weight, mask, place, row, first):
        cols = weight.shape[1]

        def rows(i, carry):
            span = pl.ds(pl.multiple_of(i * TILE, TILE), TILE)
            into = pl.ds(pl.multiple_of(row + i * TILE, TILE), TILE)
            for j in range(cols // TILE):
                at = slice(j * TILE, (j + 1) * TILE)
                to = slice(first + j * TILE, first + (j + 1) * TILE)
                bound = slice(place + j * TILE, place + (j + 1) * TILE)
                keep = mask[i, j].astype(F32)
                w = weight[span, at].astype(F32)
                top, most = bounds[0:1, bound], bounds[1:2, bound]
                coded[into, to] = (jnp.clip(w, -top, top) * keep).astype(BF16)
                inside[into, to] = jnp.where(jnp.abs(w) <= most, keep, 0.0).astype(BF16)
            return carry

        lax.fori_loop(0, weight.shape[0] // TILE, rows, 0)

    cols = w_gate.shape[1]
    one(w_gate, mask_gate, 0, 0, 0)
    one(w_up, mask_up, cols, 0, cols)
    one(w_down, mask_down, 2 * cols, w_gate.shape[0], 0)


def quantize(w_gate, w_up, w_down, e_gate, e_up, e_down, mask_gate, mask_up, mask_down):
    both = jax.ShapeDtypeStruct((w_gate.shape[0] + w_down.shape[0], w_down.shape[1]), BF16)
    found = [limits(e_gate, D), limits(e_up, D), limits(e_down, F)]
    bounds = jnp.stack([jnp.concatenate(row) for row in zip(*found)])
    smem = pl.BlockSpec(memory_space=pltpu.SMEM)
    vmem = pl.BlockSpec(memory_space=pltpu.VMEM)
    return pl.pallas_call(
        quantize_kernel,
        out_shape=(both, both),
        in_specs=[smem] * 3 + [vmem] * 4,
        out_specs=(vmem, vmem),
        compiler_params=pltpu.CompilerParams(vmem_limit_bytes=32 << 20),
    )(mask_gate, mask_up, mask_down, w_gate, w_up, w_down, bounds)


def dot(left, right, left_dim, right_dim):
    return lax.dot_general(
        left, right, (((left_dim,), (right_dim,)), ((), ())), preferred_element_type=F32
    )


def shift(block, axis, step):
    if axis == "x":
        size, inner = 4, 2
        names = "depth"
    else:
        size, inner = lax.axis_size(axis), 8
        names = (axis, "depth")
    pairs = [
        (i * inner + d, (i + (-step if d % 2 else step)) % size * inner + d)
        for i in range(size)
        for d in range(inner)
    ]
    return lax.ppermute(block, names, pairs)


def swap(block):
    return lax.ppermute(block, "depth", [(i, i ^ 1) for i in range(8)])


def together(*values):
    return lax.optimization_barrier(values)


def gather_x(block):
    ahead, behind = shift(block, "x", -1), shift(block, "x", 1)
    return [block, ahead, shift(behind, "x", 1), behind]


def scatter_x(parts):
    up = shift(parts[2].astype(BF16), "x", 1).astype(F32)
    up = shift((parts[1] + up).astype(BF16), "x", 1).astype(F32)
    down = shift(parts[3].astype(BF16), "x", -1).astype(F32)
    return parts[0] + up + down


def stack_rows(place, blocks):
    rows, cols = blocks[0].shape
    slab = cols // 2

    def kernel(place, *refs):
        near, far = refs[4:]
        for j in range(4):
            at = pl.ds(pl.multiple_of(place[j] * rows, rows), rows)
            near[at, :] = refs[j][:, :slab]
            far[at, :] = refs[j][:, slab:]

    half = jax.ShapeDtypeStruct((4 * rows, slab), BF16)
    vmem = pl.BlockSpec(memory_space=pltpu.VMEM)
    return pl.pallas_call(
        kernel,
        out_shape=(half, half),
        in_specs=[pl.BlockSpec(memory_space=pltpu.SMEM)] + [vmem] * 4,
        out_specs=(vmem, vmem),
        compiler_params=pltpu.CompilerParams(vmem_limit_bytes=32 << 20),
    )(jnp.stack(place).astype(jnp.int32), *blocks)


def stack_cols(blocks):
    _, rows, cols = blocks[0].shape
    slab = cols // 2

    def kernel(*refs):
        near, far = refs[8:]
        for k in range(8):
            for p in range(4):
                at = slice((p * 8 + k) * rows, (p * 8 + k + 1) * rows)
                near[at, :] = refs[k][p, :, :slab]
                far[at, :] = refs[k][p, :, slab:]

    half = jax.ShapeDtypeStruct((32 * rows, slab), BF16)
    vmem = pl.BlockSpec(memory_space=pltpu.VMEM)
    return pl.pallas_call(
        kernel,
        out_shape=(half, half),
        in_specs=[vmem] * 8,
        out_specs=(vmem, vmem),
        compiler_params=pltpu.CompilerParams(vmem_limit_bytes=32 << 20),
    )(*blocks)


def gather(own_t, own_g, place, quantized):
    slabs = own_t.shape[1]
    t4 = shift(own_t, "col", 4)
    near = [own_g, shift(own_g, "row", -1), shift(own_g, "row", 2), shift(own_g, "row", 1)]
    tall = jnp.zeros((4, 16, slabs), BF16)
    for j, block in enumerate(near):
        tall = lax.dynamic_update_slice(tall, block[None], (place[j], 0, 0))
    t4, tall = together(t4, tall)
    got = shift(jnp.stack([own_t, t4]), "col", -2)
    g1, g7 = shift(tall, "col", -1), shift(tall, "col", 1)
    got, g1, g7 = together(got, g1, g7)
    even = jnp.stack([own_t, got[0], t4, got[1]])
    odd = shift(even, "col", -1)
    g2, g6 = shift(g1, "col", -1), shift(g7, "col", 1)
    odd, g2, g6 = together(odd, g2, g6)
    wide = jnp.stack([even, odd], axis=1).reshape(128, slabs)
    t1, t3 = shift(wide, "row", -1), shift(wide, "row", 1)
    g3, g5 = shift(g2, "col", -1), shift(g6, "col", 1)
    coded, inside = quantized(odd)
    t3, coded, inside = together(t3, coded, inside)
    t2, g4 = shift(t3, "row", 1), shift(g5, "col", 1)
    t = stack_rows(place, [wide, t1, t2, t3])
    g = stack_cols([tall, g1, g2, g3, g4, g5, g6, g7])
    return t, g, coded, inside


def scatter(out, back, place, units, far_units, grads):
    def send(part, axis, step, wire=BF16):
        return shift(part.astype(wire), axis, step).astype(F32)

    o1, b1 = send(out[2], "row", 1), send(back[4], "col", 1)
    o1, b1, out3, back5 = together(o1, b1, out[3], back[5])
    o1, o3 = send(out[1] + o1, "row", 1), send(out3, "row", -1)
    b1, b7 = send(back[3] + b1, "col", 1), send(back5, "col", -1)
    o1, o3, b1, b7, units, far_units = together(o1, o3, b1, b7, units, far_units)
    sums = (out[0] + o1 + o3).reshape(4, 2, 16, out[0].shape[1])
    got = send(sums[:, 1], "col", 1)
    b1, b7 = send(back[2] + b1, "col", 1), send(back[6] + b7, "col", -1)
    grad_gate = grads[0](units, far_units)
    got, b1, b7, grad_gate, units, far_units = together(got, b1, b7, grad_gate, units, far_units)
    even = sums[:, 0] + got
    got = send(even[1::2], "col", 2)
    b1, b7 = send(back[1] + b1, "col", 1), send(back[7] + b7, "col", -1)
    grad_up = grads[1](units, far_units)
    got, b1, b7, grad_up, units, far_units = together(got, b1, b7, grad_up, units, far_units)
    near = even[::2] + got
    out = near[0] + send(near[1], "col", 4)
    back = back[0] + b1 + b7
    parts = [lax.dynamic_index_in_dim(back, at, 0, keepdims=False) for at in place]
    back = (
        parts[0]
        + send(parts[1], "row", 1, F32)
        + send(parts[3], "row", -1, F32)
        + send(parts[2], "row", 2, F32)
    )
    grad_down = grads[2](units, far_units)
    out, back, grad_down = together(out, back, grad_down)
    return out, back, (grad_gate, grad_up, grad_down)


def unit_backward(d_act, gate, up, sig):
    d_gate = (d_act * up * sig * (1.0 + gate * (1.0 - sig))).astype(jnp.bfloat16)
    d_up = (d_act * gate * sig).astype(jnp.bfloat16)
    return (d_gate, d_up)


def shards(
    tokens,
    grad_out,
    w_gate,
    w_up,
    w_down,
    exp_gate,
    exp_up,
    exp_down,
    mask_gate,
    mask_up,
    mask_down,
):
    depth = lax.axis_index("depth")
    x, core = depth // 2, depth % 2
    slab = tokens.shape[1]

    pair = jnp.concatenate([tokens, grad_out], axis=1)
    kept = lax.dynamic_slice_in_dim(pair, core * 16, 16, 0)
    got = swap(lax.dynamic_slice_in_dim(pair, (1 - core) * 16, 16, 0))
    own_t = jnp.concatenate([kept[:, :slab], got[:, :slab]], axis=1)
    own_g = jnp.concatenate([kept[:, slab:], got[:, slab:]], axis=1)

    place = [(jnp.where(core == 0, j - x, x - j) + 4) % 4 for j in range(4)]

    def quantized(early):
        small = together(exp_gate, exp_up, exp_down, mask_gate, mask_up, mask_down, early)[:6]
        return quantize(w_gate, w_up, w_down, *small)

    (near_t, away_t), (near_g, away_g), coded, inside = gather(own_t, own_g, place, quantized)
    coded_far = swap(coded)
    far_t, far_g = swap(away_t), swap(away_g)

    def partial(first, rows):
        at = slice(first, first + rows)
        gate_up = dot(near_t[at], coded[:slab], 1, 0) + dot(away_t[at], coded_far[:slab], 1, 0)
        d_act = dot(near_g[at], coded[slab:], 1, 1) + dot(away_g[at], coded_far[slab:], 1, 1)
        return gate_up, d_act

    far_part = jnp.concatenate(partial(256, 128), axis=1)
    gate_up, d_act = partial(0, 512)
    parts = [
        jnp.concatenate([gate_up[s : s + 128], d_act[s : s + 128]], axis=1) for s in (0, 128, 384)
    ]
    total = scatter_x([*parts[:2], far_part, parts[2]])
    total = together(total, far_t, far_g)[0]
    gate, up, d_act = total[:, :512], total[:, 512:1024], total[:, 1024:]
    sig = jax.nn.sigmoid(gate)
    act = (gate * sig * up).astype(BF16)
    d_gate, d_up = unit_backward(d_act, gate, up, sig)
    own = jnp.concatenate([act, d_gate, d_up], axis=1)
    units = jnp.concatenate(gather_x(own), axis=0)

    far_units = swap(units)

    def out_part(j):
        rows = lax.dynamic_slice_in_dim(units[:, :512], place[j] * 128, 128, 0)
        return jnp.concatenate(
            [dot(rows, coded[slab:], 1, 0), dot(rows, coded_far[slab:], 1, 0)], axis=1
        )

    def back_part(rows):
        return jnp.concatenate(
            [dot(rows, coded[:slab], 1, 1), dot(rows, coded_far[:slab], 1, 1)], axis=1
        )

    both = units[:, 512:]
    back_far = back_part(both.reshape(4, 8, 16, 1024)[:, 4].reshape(64, 1024))
    out = [out_part(j) for j in range(4)]
    back = back_part(both).reshape(4, 8, 16, 2 * slab)
    back = [back[:, k] for k in range(8)]
    back[4] = back_far.reshape(4, 16, 2 * slab)

    def unit_grad(columns, mask):
        def grad(units, far_units):
            sums = dot(near_t, units[:, columns], 0, 0) + dot(far_t, far_units[:, columns], 0, 0)
            return sums * mask.astype(F32)

        return grad

    def down_grad(units, far_units):
        sums = dot(units[:, :512], near_g, 0, 0) + dot(far_units[:, :512], far_g, 0, 0)
        return sums * inside[slab:].astype(F32)

    out, back, grads = scatter(
        out,
        back,
        place,
        units,
        far_units,
        [
            unit_grad(slice(512, 1024), inside[:slab, :512]),
            unit_grad(slice(1024, 1536), inside[:slab, 512:]),
            down_grad,
        ],
    )

    out, back = out.astype(BF16), back.astype(BF16)
    got = swap(jnp.concatenate([out[:, slab:], back[:, slab:]], axis=1))

    def finish(mine, other):
        return jnp.where(
            core == 0,
            jnp.concatenate([mine, other], axis=0),
            jnp.concatenate([other, mine], axis=0),
        )

    out = finish(out[:, :slab], got[:, :slab])
    back = finish(back[:, :slab], got[:, slab:])
    return (out, back, *grads)


def solution(mesh):
    in_specs = (
        P(("row", "col"), "depth"),
        P(("row", "col"), "depth"),
        P("depth", ("row", "col")),
        P("depth", ("row", "col")),
        P(("row", "col"), "depth"),
        P(("row", "col")),
        P(("row", "col")),
        P("depth"),
        P("depth", ("row", "col")),
        P("depth", ("row", "col")),
        P(("row", "col"), "depth"),
    )
    out_specs = (
        P(("row", "col"), "depth"),
        P(("row", "col"), "depth"),
        P("depth", ("row", "col")),
        P("depth", ("row", "col")),
        P(("row", "col"), "depth"),
    )
    return jax.shard_map(shards, mesh=mesh, in_specs=in_specs, out_specs=out_specs, check_vma=False)
```

```python
import jax
import jax.numpy as jnp
from jax import lax
from jax.experimental import pallas as pl
from jax.experimental.pallas import tpu as pltpu
from jax.sharding import PartitionSpec as P

D = 8192
F = 16384
TILE = 128
BF16 = jnp.bfloat16
F32 = jnp.float32


def limits(exponent, fan_in):
    offset = fan_in.bit_length() // 2
    scale = jnp.exp2(exponent.astype(F32) - float(offset))
    top = 127.0 / jnp.left_shift(1, offset - exponent).astype(F32)
    return top, jnp.where(jnp.abs(top / scale) <= 127.0, top, top * (1.0 - 2.0**-9))


def quantize_kernel(mask_gate, mask_up, mask_down, w_gate, w_up, w_down, bounds, coded, inside):
    def one(weight, mask, place, row, first):
        cols = weight.shape[1]

        def rows(i, carry):
            span = pl.ds(pl.multiple_of(i * TILE, TILE), TILE)
            into = pl.ds(pl.multiple_of(row + i * TILE, TILE), TILE)
            for j in range(cols // TILE):
                at = slice(j * TILE, (j + 1) * TILE)
                to = slice(first + j * TILE, first + (j + 1) * TILE)
                bound = slice(place + j * TILE, place + (j + 1) * TILE)
                keep = mask[i, j].astype(F32)
                w = weight[span, at].astype(F32)
                top, most = bounds[0:1, bound], bounds[1:2, bound]
                coded[into, to] = (jnp.clip(w, -top, top) * keep).astype(BF16)
                inside[into, to] = jnp.where(jnp.abs(w) <= most, keep, 0.0).astype(BF16)
            return carry

        lax.fori_loop(0, weight.shape[0] // TILE, rows, 0)

    cols = w_gate.shape[1]
    one(w_gate, mask_gate, 0, 0, 0)
    one(w_up, mask_up, cols, 0, cols)
    one(w_down, mask_down, 2 * cols, w_gate.shape[0], 0)


def quantize(w_gate, w_up, w_down, e_gate, e_up, e_down, mask_gate, mask_up, mask_down):
    both = jax.ShapeDtypeStruct((w_gate.shape[0] + w_down.shape[0], w_down.shape[1]), BF16)
    found = [limits(e_gate, D), limits(e_up, D), limits(e_down, F)]
    bounds = jnp.stack([jnp.concatenate(row) for row in zip(*found)])
    smem = pl.BlockSpec(memory_space=pltpu.SMEM)
    vmem = pl.BlockSpec(memory_space=pltpu.VMEM)
    return pl.pallas_call(
        quantize_kernel,
        out_shape=(both, both),
        in_specs=[smem] * 3 + [vmem] * 4,
        out_specs=(vmem, vmem),
        compiler_params=pltpu.CompilerParams(vmem_limit_bytes=32 << 20),
    )(mask_gate, mask_up, mask_down, w_gate, w_up, w_down, bounds)


def dot(left, right, left_dim, right_dim):
    return lax.dot_general(
        left, right, (((left_dim,), (right_dim,)), ((), ())), preferred_element_type=F32
    )


def shift(block, axis, step):
    if axis == "x":
        size, inner = 4, 2
        names = "depth"
    else:
        size, inner = lax.axis_size(axis), 8
        names = (axis, "depth")
    pairs = [
        (i * inner + d, (i + (-step if d % 2 else step)) % size * inner + d)
        for i in range(size)
        for d in range(inner)
    ]
    return lax.ppermute(block, names, pairs)


def swap(block):
    return lax.ppermute(block, "depth", [(i, i ^ 1) for i in range(8)])


def together(*values):
    return lax.optimization_barrier(values)


def gather_x(block):
    ahead, behind = shift(block, "x", -1), shift(block, "x", 1)
    return [block, ahead, shift(behind, "x", 1), behind]


def scatter_x(parts):
    up = shift(parts[2].astype(BF16), "x", 1).astype(F32)
    up = shift((parts[1] + up).astype(BF16), "x", 1).astype(F32)
    down = shift(parts[3].astype(BF16), "x", -1).astype(F32)
    return parts[0] + up + down


def stack_rows(place, blocks):
    rows, cols = blocks[0].shape
    slab = cols // 2

    def kernel(place, *refs):
        near, far = refs[4:]
        for j in range(4):
            at = pl.ds(pl.multiple_of(place[j] * rows, rows), rows)
            near[at, :] = refs[j][:, :slab]
            far[at, :] = refs[j][:, slab:]

    half = jax.ShapeDtypeStruct((4 * rows, slab), BF16)
    vmem = pl.BlockSpec(memory_space=pltpu.VMEM)
    return pl.pallas_call(
        kernel,
        out_shape=(half, half),
        in_specs=[pl.BlockSpec(memory_space=pltpu.SMEM)] + [vmem] * 4,
        out_specs=(vmem, vmem),
        compiler_params=pltpu.CompilerParams(vmem_limit_bytes=32 << 20),
    )(jnp.stack(place).astype(jnp.int32), *blocks)


def stack_cols(blocks):
    _, rows, cols = blocks[0].shape
    slab = cols // 2

    def kernel(*refs):
        near, far = refs[8:]
        for k in range(8):
            for p in range(4):
                at = slice((p * 8 + k) * rows, (p * 8 + k + 1) * rows)
                near[at, :] = refs[k][p, :, :slab]
                far[at, :] = refs[k][p, :, slab:]

    half = jax.ShapeDtypeStruct((32 * rows, slab), BF16)
    vmem = pl.BlockSpec(memory_space=pltpu.VMEM)
    return pl.pallas_call(
        kernel,
        out_shape=(half, half),
        in_specs=[vmem] * 8,
        out_specs=(vmem, vmem),
        compiler_params=pltpu.CompilerParams(vmem_limit_bytes=32 << 20),
    )(*blocks)


def gather(own_t, own_g, place, quantized):
    slabs = own_t.shape[1]
    t4 = shift(own_t, "col", 4)
    near = [own_g, shift(own_g, "row", -1), shift(own_g, "row", 2), shift(own_g, "row", 1)]
    tall = jnp.zeros((4, 16, slabs), BF16)
    for j, block in enumerate(near):
        tall = lax.dynamic_update_slice(tall, block[None], (place[j], 0, 0))
    t4, tall = together(t4, tall)
    ride = jnp.concatenate([tall, jnp.stack([own_t, t4])])
    r1, r7 = shift(ride, "col", -1), shift(ride, "col", 1)
    r1, r7 = together(r1, r7)
    r2, g6 = shift(r1, "col", -1), shift(r7[:4], "col", 1)
    r2, g6 = together(r2, g6)
    g1, g2, g7 = r1[:4], r2[:4], r7[:4]
    wide = [own_t, r1[4], r2[4], r7[5], t4, r1[5], r2[5], r7[4]]
    wide = jnp.concatenate(wide)
    t1, t3 = shift(wide, "row", -1), shift(wide, "row", 1)
    g3, g5 = shift(g2, "col", -1), shift(g6, "col", 1)
    coded, inside = quantized(g6)
    t3, coded, inside = together(t3, coded, inside)
    t2, g4 = shift(t3, "row", 1), shift(g5, "col", 1)
    t = stack_rows(place, [wide, t1, t2, t3])
    g = stack_cols([tall, g1, g2, g3, g4, g5, g6, g7])
    return t, g, coded, inside


def scatter(out, back, place, units, far_units, grads):
    def send(part, axis, step, wire=BF16):
        return shift(part.astype(wire), axis, step).astype(F32)

    o1, b1 = send(out[2], "row", 1), send(back[4], "col", 1)
    o1, b1, out3, back5 = together(o1, b1, out[3], back[5])
    o1, o3 = send(out[1] + o1, "row", 1), send(out3, "row", -1)
    b1, b7 = send(back[3] + b1, "col", 1), send(back5, "col", -1)
    o1, o3, b1, b7, units, far_units = together(o1, o3, b1, b7, units, far_units)
    sums = (out[0] + o1 + o3).reshape(8, 16, out[0].shape[1])
    r1 = send(jnp.concatenate([back[2] + b1, jnp.stack([sums[2], sums[6]])]), "col", 1)
    b7 = send(back[6] + b7, "col", -1)
    grad_gate = grads[0](units, far_units)
    r1, b7, grad_gate, units, far_units = together(r1, b7, grad_gate, units, far_units)
    one, five = sums[1] + r1[4], sums[5] + r1[5]
    r1 = send(jnp.concatenate([back[1] + r1[:4], jnp.stack([one, five])]), "col", 1)
    r7 = send(jnp.concatenate([back[7] + b7, jnp.stack([sums[7], sums[3]])]), "col", -1)
    grad_up = grads[1](units, far_units)
    r1, r7, grad_up, units, far_units = together(r1, r7, grad_up, units, far_units)
    out = sums[0] + r1[4] + r7[4] + send(sums[4] + r1[5] + r7[5], "col", 4)
    back = back[0] + r1[:4] + r7[:4]
    parts = [lax.dynamic_index_in_dim(back, at, 0, keepdims=False) for at in place]
    back = (
        parts[0]
        + send(parts[1], "row", 1, F32)
        + send(parts[3], "row", -1, F32)
        + send(parts[2], "row", 2, F32)
    )
    grad_down = grads[2](units, far_units)
    out, back, grad_down = together(out, back, grad_down)
    return out, back, (grad_gate, grad_up, grad_down)


def unit_backward(d_act, gate, up, sig):
    d_gate = (d_act * up * sig * (1.0 + gate * (1.0 - sig))).astype(jnp.bfloat16)
    d_up = (d_act * gate * sig).astype(jnp.bfloat16)
    return (d_gate, d_up)


def shards(
    tokens,
    grad_out,
    w_gate,
    w_up,
    w_down,
    exp_gate,
    exp_up,
    exp_down,
    mask_gate,
    mask_up,
    mask_down,
):
    depth = lax.axis_index("depth")
    x, core = depth // 2, depth % 2
    slab = tokens.shape[1]

    pair = jnp.concatenate([tokens, grad_out], axis=1)
    kept = lax.dynamic_slice_in_dim(pair, core * 16, 16, 0)
    got = swap(lax.dynamic_slice_in_dim(pair, (1 - core) * 16, 16, 0))
    own_t = jnp.concatenate([kept[:, :slab], got[:, :slab]], axis=1)
    own_g = jnp.concatenate([kept[:, slab:], got[:, slab:]], axis=1)

    place = [(jnp.where(core == 0, j - x, x - j) + 4) % 4 for j in range(4)]

    def quantized(early):
        small = together(exp_gate, exp_up, exp_down, mask_gate, mask_up, mask_down, early)[:6]
        return quantize(w_gate, w_up, w_down, *small)

    (near_t, away_t), (near_g, away_g), coded, inside = gather(own_t, own_g, place, quantized)
    coded_far = swap(coded)
    far_t, far_g = swap(away_t), swap(away_g)

    def partial(first, rows):
        at = slice(first, first + rows)
        gate_up = dot(near_t[at], coded[:slab], 1, 0) + dot(away_t[at], coded_far[:slab], 1, 0)
        d_act = dot(near_g[at], coded[slab:], 1, 1) + dot(away_g[at], coded_far[slab:], 1, 1)
        return gate_up, d_act

    far_part = jnp.concatenate(partial(256, 128), axis=1)
    gate_up, d_act = partial(0, 512)
    parts = [
        jnp.concatenate([gate_up[s : s + 128], d_act[s : s + 128]], axis=1) for s in (0, 128, 384)
    ]
    total = scatter_x([*parts[:2], far_part, parts[2]])
    total = together(total, far_t, far_g)[0]
    gate, up, d_act = total[:, :512], total[:, 512:1024], total[:, 1024:]
    sig = jax.nn.sigmoid(gate)
    act = (gate * sig * up).astype(BF16)
    d_gate, d_up = unit_backward(d_act, gate, up, sig)
    own = jnp.concatenate([act, d_gate, d_up], axis=1)
    units = jnp.concatenate(gather_x(own), axis=0)

    far_units = swap(units)

    def out_part(j):
        rows = lax.dynamic_slice_in_dim(units[:, :512], place[j] * 128, 128, 0)
        return jnp.concatenate(
            [dot(rows, coded[slab:], 1, 0), dot(rows, coded_far[slab:], 1, 0)], axis=1
        )

    def back_part(rows):
        return jnp.concatenate(
            [dot(rows, coded[:slab], 1, 1), dot(rows, coded_far[:slab], 1, 1)], axis=1
        )

    both = units[:, 512:]
    back_far = back_part(both.reshape(4, 8, 16, 1024)[:, 4].reshape(64, 1024))
    out = [out_part(j) for j in range(4)]
    back = back_part(both).reshape(4, 8, 16, 2 * slab)
    back = [back[:, k] for k in range(8)]
    back[4] = back_far.reshape(4, 16, 2 * slab)

    def unit_grad(columns, mask):
        def grad(units, far_units):
            sums = dot(near_t, units[:, columns], 0, 0) + dot(far_t, far_units[:, columns], 0, 0)
            return sums * mask.astype(F32)

        return grad

    def down_grad(units, far_units):
        sums = dot(units[:, :512], near_g, 0, 0) + dot(far_units[:, :512], far_g, 0, 0)
        return sums * inside[slab:].astype(F32)

    out, back, grads = scatter(
        out,
        back,
        place,
        units,
        far_units,
        [
            unit_grad(slice(512, 1024), inside[:slab, :512]),
            unit_grad(slice(1024, 1536), inside[:slab, 512:]),
            down_grad,
        ],
    )

    out, back = out.astype(BF16), back.astype(BF16)
    got = swap(jnp.concatenate([out[:, slab:], back[:, slab:]], axis=1))

    def finish(mine, other):
        return jnp.where(
            core == 0,
            jnp.concatenate([mine, other], axis=0),
            jnp.concatenate([other, mine], axis=0),
        )

    out = finish(out[:, :slab], got[:, :slab])
    back = finish(back[:, :slab], got[:, slab:])
    return (out, back, *grads)


def solution(mesh):
    in_specs = (
        P(("row", "col"), "depth"),
        P(("row", "col"), "depth"),
        P("depth", ("row", "col")),
        P("depth", ("row", "col")),
        P(("row", "col"), "depth"),
        P(("row", "col")),
        P(("row", "col")),
        P("depth"),
        P("depth", ("row", "col")),
        P("depth", ("row", "col")),
        P(("row", "col"), "depth"),
    )
    out_specs = (
        P(("row", "col"), "depth"),
        P(("row", "col"), "depth"),
        P("depth", ("row", "col")),
        P("depth", ("row", "col")),
        P(("row", "col"), "depth"),
    )
    return jax.shard_map(shards, mesh=mesh, in_specs=in_specs, out_specs=out_specs, check_vma=False)
```

```python
import jax
import jax.numpy as jnp
from jax import lax
from jax.experimental import pallas as pl
from jax.experimental.pallas import tpu as pltpu
from jax.sharding import PartitionSpec as P

D = 8192
F = 16384
TILE = 128
BF16 = jnp.bfloat16
F32 = jnp.float32


def limits(exponent, fan_in):
    offset = fan_in.bit_length() // 2
    scale = jnp.exp2(exponent.astype(F32) - float(offset))
    top = 127.0 / jnp.left_shift(1, offset - exponent).astype(F32)
    return top, jnp.where(jnp.abs(top / scale) <= 127.0, top, top * (1.0 - 2.0**-9))


def quantize_kernel(mask_gate, mask_up, mask_down, w_gate, w_up, w_down, bounds, coded, inside):
    def one(weight, mask, place, row, first):
        cols = weight.shape[1]

        def rows(i, carry):
            span = pl.ds(pl.multiple_of(i * TILE, TILE), TILE)
            into = pl.ds(pl.multiple_of(row + i * TILE, TILE), TILE)
            for j in range(cols // TILE):
                at = slice(j * TILE, (j + 1) * TILE)
                to = slice(first + j * TILE, first + (j + 1) * TILE)
                bound = slice(place + j * TILE, place + (j + 1) * TILE)
                keep = mask[i, j].astype(F32)
                w = weight[span, at].astype(F32)
                top, most = bounds[0:1, bound], bounds[1:2, bound]
                coded[into, to] = (jnp.clip(w, -top, top) * keep).astype(BF16)
                inside[into, to] = jnp.where(jnp.abs(w) <= most, keep, 0.0).astype(BF16)
            return carry

        lax.fori_loop(0, weight.shape[0] // TILE, rows, 0)

    cols = w_gate.shape[1]
    one(w_gate, mask_gate, 0, 0, 0)
    one(w_up, mask_up, cols, 0, cols)
    one(w_down, mask_down, 2 * cols, w_gate.shape[0], 0)


def quantize(w_gate, w_up, w_down, e_gate, e_up, e_down, mask_gate, mask_up, mask_down):
    both = jax.ShapeDtypeStruct((w_gate.shape[0] + w_down.shape[0], w_down.shape[1]), BF16)
    found = [limits(e_gate, D), limits(e_up, D), limits(e_down, F)]
    bounds = jnp.stack([jnp.concatenate(row) for row in zip(*found)])
    smem = pl.BlockSpec(memory_space=pltpu.SMEM)
    vmem = pl.BlockSpec(memory_space=pltpu.VMEM)
    return pl.pallas_call(
        quantize_kernel,
        out_shape=(both, both),
        in_specs=[smem] * 3 + [vmem] * 4,
        out_specs=(vmem, vmem),
        compiler_params=pltpu.CompilerParams(vmem_limit_bytes=32 << 20),
    )(mask_gate, mask_up, mask_down, w_gate, w_up, w_down, bounds)


def dot(left, right, left_dim, right_dim):
    return lax.dot_general(
        left, right, (((left_dim,), (right_dim,)), ((), ())), preferred_element_type=F32
    )


def shift(block, axis, step):
    if axis == "x":
        size, inner = 4, 2
        names = "depth"
    else:
        size, inner = lax.axis_size(axis), 8
        names = (axis, "depth")
    pairs = [
        (i * inner + d, (i + (-step if d % 2 else step)) % size * inner + d)
        for i in range(size)
        for d in range(inner)
    ]
    return lax.ppermute(block, names, pairs)


def swap(block):
    return lax.ppermute(block, "depth", [(i, i ^ 1) for i in range(8)])


def together(*values):
    return lax.optimization_barrier(values)


def gather_x(block):
    ahead, behind = shift(block, "x", -1), shift(block, "x", 1)
    return [block, ahead, shift(behind, "x", 1), behind]


def scatter_x(parts):
    up = shift(parts[2].astype(BF16), "x", 1).astype(F32)
    up = shift((parts[1] + up).astype(BF16), "x", 1).astype(F32)
    down = shift(parts[3].astype(BF16), "x", -1).astype(F32)
    return parts[0] + up + down


def stack_rows(place, blocks):
    rows, cols = blocks[0].shape
    slab = cols // 2

    def kernel(place, *refs):
        near, far = refs[4:]
        for j in range(4):
            at = pl.ds(pl.multiple_of(place[j] * rows, rows), rows)
            near[at, :] = refs[j][:, :slab]
            far[at, :] = refs[j][:, slab:]

    half = jax.ShapeDtypeStruct((4 * rows, slab), BF16)
    vmem = pl.BlockSpec(memory_space=pltpu.VMEM)
    return pl.pallas_call(
        kernel,
        out_shape=(half, half),
        in_specs=[pl.BlockSpec(memory_space=pltpu.SMEM)] + [vmem] * 4,
        out_specs=(vmem, vmem),
        compiler_params=pltpu.CompilerParams(vmem_limit_bytes=32 << 20),
    )(jnp.stack(place).astype(jnp.int32), *blocks)


def stack_wide(own, four, first, second, behind):
    rows, cols = own.shape

    def kernel(own, four, first, second, behind, out):
        out[0:rows, :] = own[...]
        out[4 * rows : 5 * rows, :] = four[...]
        for k, (block, at) in {
            1: (first, 4),
            2: (second, 4),
            3: (behind, 5),
            5: (first, 5),
            6: (second, 5),
            7: (behind, 4),
        }.items():
            out[k * rows : (k + 1) * rows, :] = block[at]

    vmem = pl.BlockSpec(memory_space=pltpu.VMEM)
    return pl.pallas_call(
        kernel,
        out_shape=jax.ShapeDtypeStruct((8 * rows, cols), BF16),
        in_specs=[vmem] * 5,
        out_specs=vmem,
        compiler_params=pltpu.CompilerParams(vmem_limit_bytes=32 << 20),
    )(own, four, first, second, behind)


def stack_cols(blocks):
    _, rows, cols = blocks[0].shape
    slab = cols // 2

    def kernel(*refs):
        near, far = refs[8:]
        for k in range(8):
            for p in range(4):
                at = slice((p * 8 + k) * rows, (p * 8 + k + 1) * rows)
                near[at, :] = refs[k][p, :, :slab]
                far[at, :] = refs[k][p, :, slab:]

    half = jax.ShapeDtypeStruct((32 * rows, slab), BF16)
    vmem = pl.BlockSpec(memory_space=pltpu.VMEM)
    return pl.pallas_call(
        kernel,
        out_shape=(half, half),
        in_specs=[vmem] * 8,
        out_specs=(vmem, vmem),
        compiler_params=pltpu.CompilerParams(vmem_limit_bytes=32 << 20),
    )(*blocks)


def gather(own_t, own_g, place, quantized):
    slabs = own_t.shape[1]
    t4 = shift(own_t, "col", 4)
    near = [own_g, shift(own_g, "row", -1), shift(own_g, "row", 2), shift(own_g, "row", 1)]
    tall = jnp.zeros((4, 16, slabs), BF16)
    for j, block in enumerate(near):
        tall = lax.dynamic_update_slice(tall, block[None], (place[j], 0, 0))
    t4, tall = together(t4, tall)
    ride = jnp.concatenate([tall, jnp.stack([own_t, t4])])
    r1, r7 = shift(ride, "col", -1), shift(ride, "col", 1)
    r1, r7 = together(r1, r7)
    r2, g6 = shift(r1, "col", -1), shift(r7[:4], "col", 1)
    r2, g6 = together(r2, g6)
    g1, g2, g7 = r1[:4], r2[:4], r7[:4]
    wide = stack_wide(own_t, t4, r1, r2, r7)
    t1, t3 = shift(wide, "row", -1), shift(wide, "row", 1)
    g3, g5 = shift(g2, "col", -1), shift(g6, "col", 1)
    coded, inside = quantized(g6)
    t3, coded, inside = together(t3, coded, inside)
    t2, g4 = shift(t3, "row", 1), shift(g5, "col", 1)
    t = stack_rows(place, [wide, t1, t2, t3])
    g = stack_cols([tall, g1, g2, g3, g4, g5, g6, g7])
    return t, g, coded, inside


def scatter(out, back, place, units, far_units, grads):
    def send(part, axis, step, wire=BF16):
        return shift(part.astype(wire), axis, step).astype(F32)

    o1, b1 = send(out[2], "row", 1), send(back[4], "col", 1)
    o1, b1, out3, back5 = together(o1, b1, out[3], back[5])
    o1, o3 = send(out[1] + o1, "row", 1), send(out3, "row", -1)
    b1, b7 = send(back[3] + b1, "col", 1), send(back5, "col", -1)
    o1, o3, b1, b7, units, far_units = together(o1, o3, b1, b7, units, far_units)
    sums = (out[0] + o1 + o3).reshape(8, 16, out[0].shape[1])
    r1 = send(jnp.concatenate([back[2] + b1, jnp.stack([sums[2], sums[6]])]), "col", 1)
    b7 = send(back[6] + b7, "col", -1)
    grad_gate = grads[0](units, far_units)
    r1, b7, grad_gate, units, far_units = together(r1, b7, grad_gate, units, far_units)
    one, five = sums[1] + r1[4], sums[5] + r1[5]
    r1 = send(jnp.concatenate([back[1] + r1[:4], jnp.stack([one, five])]), "col", 1)
    r7 = send(jnp.concatenate([back[7] + b7, jnp.stack([sums[7], sums[3]])]), "col", -1)
    grad_up = grads[1](units, far_units)
    r1, r7, grad_up, units, far_units = together(r1, r7, grad_up, units, far_units)
    out = sums[0] + r1[4] + r7[4] + send(sums[4] + r1[5] + r7[5], "col", 4)
    back = back[0] + r1[:4] + r7[:4]
    parts = [lax.dynamic_index_in_dim(back, at, 0, keepdims=False) for at in place]
    back = (
        parts[0]
        + send(parts[1], "row", 1, F32)
        + send(parts[3], "row", -1, F32)
        + send(parts[2], "row", 2, F32)
    )
    grad_down = grads[2](units, far_units)
    out, back, grad_down = together(out, back, grad_down)
    return out, back, (grad_gate, grad_up, grad_down)


def unit_backward(d_act, gate, up, sig):
    d_gate = (d_act * up * sig * (1.0 + gate * (1.0 - sig))).astype(jnp.bfloat16)
    d_up = (d_act * gate * sig).astype(jnp.bfloat16)
    return (d_gate, d_up)


def shards(
    tokens,
    grad_out,
    w_gate,
    w_up,
    w_down,
    exp_gate,
    exp_up,
    exp_down,
    mask_gate,
    mask_up,
    mask_down,
):
    depth = lax.axis_index("depth")
    x, core = depth // 2, depth % 2
    slab = tokens.shape[1]

    pair = jnp.concatenate([tokens, grad_out], axis=1)
    kept = lax.dynamic_slice_in_dim(pair, core * 16, 16, 0)
    got = swap(lax.dynamic_slice_in_dim(pair, (1 - core) * 16, 16, 0))
    own_t = jnp.concatenate([kept[:, :slab], got[:, :slab]], axis=1)
    own_g = jnp.concatenate([kept[:, slab:], got[:, slab:]], axis=1)

    place = [(jnp.where(core == 0, j - x, x - j) + 4) % 4 for j in range(4)]

    def quantized(early):
        small = together(exp_gate, exp_up, exp_down, mask_gate, mask_up, mask_down, early)[:6]
        return quantize(w_gate, w_up, w_down, *small)

    (near_t, away_t), (near_g, away_g), coded, inside = gather(own_t, own_g, place, quantized)
    coded_far = swap(coded)
    far_t, far_g = swap(away_t), swap(away_g)

    def partial(first, rows):
        at = slice(first, first + rows)
        gate_up = dot(near_t[at], coded[:slab], 1, 0) + dot(away_t[at], coded_far[:slab], 1, 0)
        d_act = dot(near_g[at], coded[slab:], 1, 1) + dot(away_g[at], coded_far[slab:], 1, 1)
        return gate_up, d_act

    far_part = jnp.concatenate(partial(256, 128), axis=1)
    gate_up, d_act = partial(0, 512)
    parts = [
        jnp.concatenate([gate_up[s : s + 128], d_act[s : s + 128]], axis=1) for s in (0, 128, 384)
    ]
    total = scatter_x([*parts[:2], far_part, parts[2]])
    total = together(total, far_t, far_g)[0]
    gate, up, d_act = total[:, :512], total[:, 512:1024], total[:, 1024:]
    sig = jax.nn.sigmoid(gate)
    act = (gate * sig * up).astype(BF16)
    d_gate, d_up = unit_backward(d_act, gate, up, sig)
    own = jnp.concatenate([act, d_gate, d_up], axis=1)
    units = jnp.concatenate(gather_x(own), axis=0)

    far_units = swap(units)

    def out_part(j):
        rows = lax.dynamic_slice_in_dim(units[:, :512], place[j] * 128, 128, 0)
        return jnp.concatenate(
            [dot(rows, coded[slab:], 1, 0), dot(rows, coded_far[slab:], 1, 0)], axis=1
        )

    def back_part(rows):
        return jnp.concatenate(
            [dot(rows, coded[:slab], 1, 1), dot(rows, coded_far[:slab], 1, 1)], axis=1
        )

    both = units[:, 512:]
    back_far = back_part(both.reshape(4, 8, 16, 1024)[:, 4].reshape(64, 1024))
    out = [out_part(j) for j in range(4)]
    back = back_part(both).reshape(4, 8, 16, 2 * slab)
    back = [back[:, k] for k in range(8)]
    back[4] = back_far.reshape(4, 16, 2 * slab)

    def unit_grad(columns, mask):
        def grad(units, far_units):
            sums = dot(near_t, units[:, columns], 0, 0) + dot(far_t, far_units[:, columns], 0, 0)
            return sums * mask.astype(F32)

        return grad

    def down_grad(units, far_units):
        sums = dot(units[:, :512], near_g, 0, 0) + dot(far_units[:, :512], far_g, 0, 0)
        return sums * inside[slab:].astype(F32)

    out, back, grads = scatter(
        out,
        back,
        place,
        units,
        far_units,
        [
            unit_grad(slice(512, 1024), inside[:slab, :512]),
            unit_grad(slice(1024, 1536), inside[:slab, 512:]),
            down_grad,
        ],
    )

    out, back = out.astype(BF16), back.astype(BF16)
    got = swap(jnp.concatenate([out[:, slab:], back[:, slab:]], axis=1))

    def finish(mine, other):
        return jnp.where(
            core == 0,
            jnp.concatenate([mine, other], axis=0),
            jnp.concatenate([other, mine], axis=0),
        )

    out = finish(out[:, :slab], got[:, :slab])
    back = finish(back[:, :slab], got[:, slab:])
    return (out, back, *grads)


def solution(mesh):
    in_specs = (
        P(("row", "col"), "depth"),
        P(("row", "col"), "depth"),
        P("depth", ("row", "col")),
        P("depth", ("row", "col")),
        P(("row", "col"), "depth"),
        P(("row", "col")),
        P(("row", "col")),
        P("depth"),
        P("depth", ("row", "col")),
        P("depth", ("row", "col")),
        P(("row", "col"), "depth"),
    )
    out_specs = (
        P(("row", "col"), "depth"),
        P(("row", "col"), "depth"),
        P("depth", ("row", "col")),
        P("depth", ("row", "col")),
        P(("row", "col"), "depth"),
    )
    return jax.shard_map(shards, mesh=mesh, in_specs=in_specs, out_specs=out_specs, check_vma=False)
```

```python
import jax
import jax.numpy as jnp
from jax import lax
from jax.experimental import pallas as pl
from jax.experimental.pallas import tpu as pltpu
from jax.sharding import PartitionSpec as P

D = 8192
F = 16384
TILE = 128
BF16 = jnp.bfloat16
F32 = jnp.float32


def limits(exponent, fan_in):
    offset = fan_in.bit_length() // 2
    scale = jnp.exp2(exponent.astype(F32) - float(offset))
    top = 127.0 / jnp.left_shift(1, offset - exponent).astype(F32)
    return top, jnp.where(jnp.abs(top / scale) <= 127.0, top, top * (1.0 - 2.0**-9))


def quantize_kernel(mask_gate, mask_up, mask_down, w_gate, w_up, w_down, bounds, coded, inside):
    def one(weight, mask, place, row, first):
        cols = weight.shape[1]

        def rows(i, carry):
            span = pl.ds(pl.multiple_of(i * TILE, TILE), TILE)
            into = pl.ds(pl.multiple_of(row + i * TILE, TILE), TILE)
            for j in range(cols // TILE):
                at = slice(j * TILE, (j + 1) * TILE)
                to = slice(first + j * TILE, first + (j + 1) * TILE)
                bound = slice(place + j * TILE, place + (j + 1) * TILE)
                keep = mask[i, j].astype(F32)
                w = weight[span, at].astype(F32)
                top, most = bounds[0:1, bound], bounds[1:2, bound]
                coded[into, to] = (jnp.clip(w, -top, top) * keep).astype(BF16)
                inside[into, to] = jnp.where(jnp.abs(w) <= most, keep, 0.0).astype(BF16)
            return carry

        lax.fori_loop(0, weight.shape[0] // TILE, rows, 0)

    cols = w_gate.shape[1]
    one(w_gate, mask_gate, 0, 0, 0)
    one(w_up, mask_up, cols, 0, cols)
    one(w_down, mask_down, 2 * cols, w_gate.shape[0], 0)


def quantize(w_gate, w_up, w_down, e_gate, e_up, e_down, mask_gate, mask_up, mask_down):
    both = jax.ShapeDtypeStruct((w_gate.shape[0] + w_down.shape[0], w_down.shape[1]), BF16)
    found = [limits(e_gate, D), limits(e_up, D), limits(e_down, F)]
    bounds = jnp.stack([jnp.concatenate(row) for row in zip(*found)])
    smem = pl.BlockSpec(memory_space=pltpu.SMEM)
    vmem = pl.BlockSpec(memory_space=pltpu.VMEM)
    return pl.pallas_call(
        quantize_kernel,
        out_shape=(both, both),
        in_specs=[smem] * 3 + [vmem] * 4,
        out_specs=(vmem, vmem),
        compiler_params=pltpu.CompilerParams(vmem_limit_bytes=32 << 20),
    )(mask_gate, mask_up, mask_down, w_gate, w_up, w_down, bounds)


def dot(left, right, left_dim, right_dim):
    return lax.dot_general(
        left, right, (((left_dim,), (right_dim,)), ((), ())), preferred_element_type=F32
    )


def shift(block, axis, step):
    if axis == "x":
        size, inner = 4, 2
        names = "depth"
    else:
        size, inner = lax.axis_size(axis), 8
        names = (axis, "depth")
    pairs = [
        (i * inner + d, (i + (-step if d % 2 else step)) % size * inner + d)
        for i in range(size)
        for d in range(inner)
    ]
    return lax.ppermute(block, names, pairs)


def swap(block):
    return lax.ppermute(block, "depth", [(i, i ^ 1) for i in range(8)])


def together(*values):
    return lax.optimization_barrier(values)


def gather_x(block):
    ahead, behind = shift(block, "x", -1), shift(block, "x", 1)
    return [block, ahead, shift(behind, "x", 1), behind]


def scatter_x(parts):
    up = shift(parts[2].astype(BF16), "x", 1).astype(F32)
    up = shift((parts[1] + up).astype(BF16), "x", 1).astype(F32)
    down = shift(parts[3].astype(BF16), "x", -1).astype(F32)
    return parts[0] + up + down


def stack_rows(place, blocks):
    rows, cols = blocks[0].shape
    slab = cols // 2

    def kernel(place, *refs):
        near, far = refs[4:]
        for j in range(4):
            at = pl.ds(pl.multiple_of(place[j] * rows, rows), rows)
            near[at, :] = refs[j][:, :slab]
            far[at, :] = refs[j][:, slab:]

    half = jax.ShapeDtypeStruct((4 * rows, slab), BF16)
    vmem = pl.BlockSpec(memory_space=pltpu.VMEM)
    return pl.pallas_call(
        kernel,
        out_shape=(half, half),
        in_specs=[pl.BlockSpec(memory_space=pltpu.SMEM)] + [vmem] * 4,
        out_specs=(vmem, vmem),
        compiler_params=pltpu.CompilerParams(vmem_limit_bytes=32 << 20),
    )(jnp.stack(place).astype(jnp.int32), *blocks)


def stack_wide(own, four, first, second, behind):
    rows, cols = own.shape

    def kernel(own, four, first, second, behind, out):
        out[0:rows, :] = own[...]
        out[4 * rows : 5 * rows, :] = four[...]
        for k, (block, at) in {
            1: (first, 4),
            2: (second, 4),
            3: (behind, 5),
            5: (first, 5),
            6: (second, 5),
            7: (behind, 4),
        }.items():
            out[k * rows : (k + 1) * rows, :] = block[at]

    vmem = pl.BlockSpec(memory_space=pltpu.VMEM)
    return pl.pallas_call(
        kernel,
        out_shape=jax.ShapeDtypeStruct((8 * rows, cols), BF16),
        in_specs=[vmem] * 5,
        out_specs=vmem,
        compiler_params=pltpu.CompilerParams(vmem_limit_bytes=32 << 20),
    )(own, four, first, second, behind)


def stack_cols(blocks):
    _, rows, cols = blocks[0].shape
    slab = cols // 2

    def kernel(*refs):
        near, far = refs[8:]
        for k in range(8):
            for p in range(4):
                at = slice((p * 8 + k) * rows, (p * 8 + k + 1) * rows)
                near[at, :] = refs[k][p, :, :slab]
                far[at, :] = refs[k][p, :, slab:]

    half = jax.ShapeDtypeStruct((32 * rows, slab), BF16)
    vmem = pl.BlockSpec(memory_space=pltpu.VMEM)
    return pl.pallas_call(
        kernel,
        out_shape=(half, half),
        in_specs=[vmem] * 8,
        out_specs=(vmem, vmem),
        compiler_params=pltpu.CompilerParams(vmem_limit_bytes=32 << 20),
    )(*blocks)


def gather(own_t, own_g, place, quantized):
    slabs = own_t.shape[1]
    t4 = shift(own_t, "col", 4)
    near = [own_g, shift(own_g, "row", -1), shift(own_g, "row", 2), shift(own_g, "row", 1)]
    tall = jnp.zeros((4, 16, slabs), BF16)
    for j, block in enumerate(near):
        tall = lax.dynamic_update_slice(tall, block[None], (place[j], 0, 0))
    t4, tall = together(t4, tall)
    ride = jnp.concatenate([tall, jnp.stack([own_t, t4])])
    r1, r7 = shift(ride, "col", -1), shift(ride, "col", 1)
    r1, r7 = together(r1, r7)
    r2, g6 = shift(r1, "col", -1), shift(r7[:4], "col", 1)
    r2, g6 = together(r2, g6)
    g1, g2, g7 = r1[:4], r2[:4], r7[:4]
    wide = stack_wide(own_t, t4, r1, r2, r7)
    t1, t3 = shift(wide, "row", -1), shift(wide, "row", 1)
    g3, g5 = shift(g2, "col", -1), shift(g6, "col", 1)
    coded, inside = quantized(g6)
    t3, g3, g5, coded, inside = together(t3, g3, g5, coded, inside)
    t2, g4 = shift(t3, "row", 1), shift(g5, "col", 1)
    t = stack_rows(place, [wide, t1, t2, t3])
    g = stack_cols([tall, g1, g2, g3, g4, g5, g6, g7])
    return t, g, coded, inside


def scatter(out, back, place, units, far_units, grads):
    def send(part, axis, step, wire=BF16):
        return shift(part.astype(wire), axis, step).astype(F32)

    o1, b1 = send(out[2], "row", 1), send(back[4], "col", 1)
    o1, b1, out3, back5 = together(o1, b1, out[3], back[5])
    o1, o3 = send(out[1] + o1, "row", 1), send(out3, "row", -1)
    b1, b7 = send(back[3] + b1, "col", 1), send(back5, "col", -1)
    o1, o3, b1, b7, units, far_units = together(o1, o3, b1, b7, units, far_units)
    sums = (out[0] + o1 + o3).reshape(8, 16, out[0].shape[1])
    r1 = send(jnp.concatenate([back[2] + b1, jnp.stack([sums[2], sums[6]])]), "col", 1)
    b7 = send(back[6] + b7, "col", -1)
    grad_gate = grads[0](units, far_units)
    r1, b7, grad_gate, units, far_units = together(r1, b7, grad_gate, units, far_units)
    one, five = sums[1] + r1[4], sums[5] + r1[5]
    r1 = send(jnp.concatenate([back[1] + r1[:4], jnp.stack([one, five])]), "col", 1)
    r7 = send(jnp.concatenate([back[7] + b7, jnp.stack([sums[7], sums[3]])]), "col", -1)
    grad_up = grads[1](units, far_units)
    r1, r7, grad_up, units, far_units = together(r1, r7, grad_up, units, far_units)
    out = sums[0] + r1[4] + r7[4] + send(sums[4] + r1[5] + r7[5], "col", 4)
    back = back[0] + r1[:4] + r7[:4]
    parts = [lax.dynamic_index_in_dim(back, at, 0, keepdims=False) for at in place]
    back = (
        parts[0]
        + send(parts[1], "row", 1, F32)
        + send(parts[3], "row", -1, F32)
        + send(parts[2], "row", 2, F32)
    )
    grad_down = grads[2](units, far_units)
    out, back, grad_down = together(out, back, grad_down)
    return out, back, (grad_gate, grad_up, grad_down)


def unit_backward(d_act, gate, up, sig):
    d_gate = (d_act * up * sig * (1.0 + gate * (1.0 - sig))).astype(jnp.bfloat16)
    d_up = (d_act * gate * sig).astype(jnp.bfloat16)
    return (d_gate, d_up)


def shards(
    tokens,
    grad_out,
    w_gate,
    w_up,
    w_down,
    exp_gate,
    exp_up,
    exp_down,
    mask_gate,
    mask_up,
    mask_down,
):
    depth = lax.axis_index("depth")
    x, core = depth // 2, depth % 2
    slab = tokens.shape[1]

    pair = jnp.concatenate([tokens, grad_out], axis=1)
    kept = lax.dynamic_slice_in_dim(pair, core * 16, 16, 0)
    got = swap(lax.dynamic_slice_in_dim(pair, (1 - core) * 16, 16, 0))
    own_t = jnp.concatenate([kept[:, :slab], got[:, :slab]], axis=1)
    own_g = jnp.concatenate([kept[:, slab:], got[:, slab:]], axis=1)

    place = [(jnp.where(core == 0, j - x, x - j) + 4) % 4 for j in range(4)]

    def quantized(early):
        small = together(exp_gate, exp_up, exp_down, mask_gate, mask_up, mask_down, early)[:6]
        return quantize(w_gate, w_up, w_down, *small)

    (near_t, away_t), (near_g, away_g), coded, inside = gather(own_t, own_g, place, quantized)
    coded_far = swap(coded)
    far_t, far_g = swap(away_t), swap(away_g)

    def partial(first, rows):
        at = slice(first, first + rows)
        gate_up = dot(near_t[at], coded[:slab], 1, 0) + dot(away_t[at], coded_far[:slab], 1, 0)
        d_act = dot(near_g[at], coded[slab:], 1, 1) + dot(away_g[at], coded_far[slab:], 1, 1)
        return gate_up, d_act

    far_part = jnp.concatenate(partial(256, 128), axis=1)
    gate_up, d_act = partial(0, 512)
    parts = [
        jnp.concatenate([gate_up[s : s + 128], d_act[s : s + 128]], axis=1) for s in (0, 128, 384)
    ]
    total = scatter_x([*parts[:2], far_part, parts[2]])
    total = together(total, far_t, far_g)[0]
    gate, up, d_act = total[:, :512], total[:, 512:1024], total[:, 1024:]
    sig = jax.nn.sigmoid(gate)
    act = (gate * sig * up).astype(BF16)
    d_gate, d_up = unit_backward(d_act, gate, up, sig)
    own = jnp.concatenate([act, d_gate, d_up], axis=1)
    units = jnp.concatenate(gather_x(own), axis=0)

    far_units = swap(units)

    def out_part(j):
        rows = lax.dynamic_slice_in_dim(units[:, :512], place[j] * 128, 128, 0)
        return jnp.concatenate(
            [dot(rows, coded[slab:], 1, 0), dot(rows, coded_far[slab:], 1, 0)], axis=1
        )

    def back_part(rows):
        return jnp.concatenate(
            [dot(rows, coded[:slab], 1, 1), dot(rows, coded_far[:slab], 1, 1)], axis=1
        )

    both = units[:, 512:]
    back_far = back_part(both.reshape(4, 8, 16, 1024)[:, 4].reshape(64, 1024))
    out = [out_part(j) for j in range(4)]
    back = back_part(both).reshape(4, 8, 16, 2 * slab)
    back = [back[:, k] for k in range(8)]
    back[4] = back_far.reshape(4, 16, 2 * slab)

    def unit_grad(columns, mask):
        def grad(units, far_units):
            sums = dot(near_t, units[:, columns], 0, 0) + dot(far_t, far_units[:, columns], 0, 0)
            return sums * mask.astype(F32)

        return grad

    def down_grad(units, far_units):
        sums = dot(units[:, :512], near_g, 0, 0) + dot(far_units[:, :512], far_g, 0, 0)
        return sums * inside[slab:].astype(F32)

    out, back, grads = scatter(
        out,
        back,
        place,
        units,
        far_units,
        [
            unit_grad(slice(512, 1024), inside[:slab, :512]),
            unit_grad(slice(1024, 1536), inside[:slab, 512:]),
            down_grad,
        ],
    )

    out, back = out.astype(BF16), back.astype(BF16)
    got = swap(jnp.concatenate([out[:, slab:], back[:, slab:]], axis=1))

    def finish(mine, other):
        return jnp.where(
            core == 0,
            jnp.concatenate([mine, other], axis=0),
            jnp.concatenate([other, mine], axis=0),
        )

    out = finish(out[:, :slab], got[:, :slab])
    back = finish(back[:, :slab], got[:, slab:])
    return (out, back, *grads)


def solution(mesh):
    in_specs = (
        P(("row", "col"), "depth"),
        P(("row", "col"), "depth"),
        P("depth", ("row", "col")),
        P("depth", ("row", "col")),
        P(("row", "col"), "depth"),
        P(("row", "col")),
        P(("row", "col")),
        P("depth"),
        P("depth", ("row", "col")),
        P("depth", ("row", "col")),
        P(("row", "col"), "depth"),
    )
    out_specs = (
        P(("row", "col"), "depth"),
        P(("row", "col"), "depth"),
        P("depth", ("row", "col")),
        P("depth", ("row", "col")),
        P(("row", "col"), "depth"),
    )
    return jax.shard_map(shards, mesh=mesh, in_specs=in_specs, out_specs=out_specs, check_vma=False)
```
